256 devices in a mesh: dp: 16 (over z, core), expert: 16 (over y, x).
Axes of the slice: x: 4, y: 4, z: 8, core: 2. Of those that a mesh axis runs over, the one named last changes fastest.
Arguments:
- tokens: bfloat16 [32768, 768], P(('dp', 'expert')), may hold values from -6 to 6
- routes: int32 [32768, 2], P(('dp', 'expert')), may hold values from 0 to 15, all different within a row; in each aligned block of 128 rows (0 to 127, 128 to 255, ...) at most 20 rows name the same one
- route_gates: float32 [32768, 2], P(('dp', 'expert')), may hold values from 0.25 to 1
- cotangent: bfloat16 [32768, 768], P(('dp', 'expert')), may hold values from -6 to 6
- gate_weight: bfloat16 [16, 3072, 768], P('expert', 'dp'), may hold values from -0.21875 to 0.21875
- up_weight: bfloat16 [16, 3072, 768], P('expert', 'dp'), may hold values from -0.21875 to 0.21875
- down_weight: bfloat16 [16, 3072, 768], P('expert', 'dp'), may hold values from -0.109375 to 0.109375
Outputs:
- mixed_output: bfloat16 [32768, 768], P(('dp', 'expert'))
- token_grads: bfloat16 [32768, 768], P(('dp', 'expert'))
- gate_grad: float32 [16, 3072, 768], P('expert', 'dp')
- up_grad: float32 [16, 3072, 768], P('expert', 'dp')
- down_grad: float32 [16, 3072, 768], P('expert', 'dp')
The draws below stay inside these ranges and needn't reach their ends.
Inputs may be any that keep to these rules, and one draw needn't show every extreme that they name: Each token names 2 different experts; no expert is named by more than 20 routes of the tokens of one device.
All inputs are finite; a program needn't handle non-finite values.
Results may differ from the reference program's by a relative error of at most 0.02.
Values may be sent and summed in bfloat16 or wider, within the bound.
No kernel may reach another device: no remote copies, remote signals or barrier semaphores. Data moves between devices by JAX's collectives and lax.ppermute only.
A program may use at most 128 MiB of HBM per device.

```python
import math
import jax
import jax.numpy as jnp
import numpy as np
from jax import lax

D = 768
FF = 3072
TOP = 2
TOK_DEV = 128
EXPERTS = 16
CAP = 20
TOKENS = 32768
N_DP = 16
N_EXPERT = 16


def level_of(own_key, extent, pieces, low, largest):
    factor_of, own = 1.0, jax.random.fold_in(own_key, 6)
    for dim, parts in pieces:
        steps = jnp.exp(jax.random.uniform(jax.random.fold_in(own, dim), (parts,), jnp.float32, low / len(pieces), largest / len(pieces)))
        factor_of = factor_of * jnp.repeat(steps, extent[dim] // parts).reshape([-1 if axis == dim else 1 for axis in range(len(extent))])
    return factor_of


def assign_block(own_key, own, number, rows, amount, top, bound, lean):
    ranking = jax.random.permutation(own_key, amount)
    heavy_load, common = portions_of(amount, rows * top, bound, lean, True), portions_of(amount, rows * top, bound, lean, False)
    places = jnp.arange(amount)

    def named(lengths, turn):
        used = int((lengths > 0).sum())
        fixed = max(1, used // 4)
        moved = fixed + (places - fixed + turn * (used - fixed)) % max(1, amount - fixed)
        return jnp.zeros((amount,), jnp.int32).at[ranking[jnp.where(places < fixed, places, moved)]].set(jnp.asarray(lengths, jnp.int32))

    lengths = jnp.where(number % 4 == 0, named(heavy_load, number // 4), named(common, number - number // 4 - 1))
    mixed = jax.random.permutation(jax.random.fold_in(own, 3), amount)
    source_of, sink = mixed[0:amount // 2 * 2:2], mixed[1:amount // 2 * 2:2]
    slack = jnp.minimum(lengths[source_of] - 1, bound - lengths[sink]) // 2
    slack = jnp.where((source_of == ranking[0]) | (sink == ranking[0]) | (lengths[sink] == 0), 0, jnp.maximum(slack, 0))
    moved = jax.random.randint(jax.random.fold_in(own, 4), (amount // 2,), 0, 1 << 20) % (slack + 1)
    lengths = lengths.at[source_of].add(-moved).at[sink].add(moved)
    items = jnp.searchsorted(jnp.cumsum(lengths), jnp.arange(rows * top), side="right").astype(jnp.int32)
    table = items.reshape(top, rows).T
    table = table[jax.random.permutation(jax.random.fold_in(own, 1), rows)]
    turn = jax.random.randint(jax.random.fold_in(own, 2), (rows, 1), 0, top)
    return jnp.take_along_axis(table, (jnp.arange(top)[None, :] + turn) % top, axis=1)


def portions_of(number_of, total, bound, skew, full):
    portions = [(1 << 20) // math.isqrt(rank ** skew) + 1 for rank in range(1, number_of + 1)]
    largest = bound if full else min(bound, max(-(-total // number_of), total * portions[0] // sum(portions)))
    least = 1 if total - largest >= number_of - 1 else 0
    given, rest = [largest] + [least] * (number_of - 1), total - largest - least * (number_of - 1)
    while rest > 0:
        free = [i for i in range(1, number_of) if given[i] < largest] or [i for i in range(1, number_of) if given[i] < bound]
        pool, remaining = sum([portions[i] for i in free]), rest
        for i in free:
            extra = min(bound - given[i], max(1, remaining * portions[i] // pool), rest)
            given[i] = given[i] + extra
            rest = rest - extra
    return np.array(given)


def noise(stream_key, dims, deviation, most, split=(), kind=jnp.bfloat16):
    gain = level_of(stream_key, dims, split, -0.22, 0.18) if split else 1.0
    entries = jax.random.normal(stream_key, dims, jnp.float32) * deviation * gain
    return jnp.minimum(jnp.maximum(entries, -most), most).astype(kind)


def setup_inputs(seed: int = 0) -> dict:
    key_of = jax.random.split(jax.random.key(seed), 8)
    tokens = noise(key_of[0], (TOKENS, D), 1.0, 6.0, ((0, 256),))
    routes_keys = jax.random.split(jax.random.fold_in(key_of[1], 1), TOKENS // TOK_DEV)
    routes_turns = jax.random.permutation(jax.random.fold_in(key_of[1], 3), TOKENS // TOK_DEV)
    routes = jax.vmap(lambda own, number: assign_block(jax.random.fold_in(key_of[1], 2), own, number, TOK_DEV, EXPERTS, TOP, CAP, 2))(routes_keys, routes_turns).reshape((TOKENS, TOP))
    route_gates = jnp.clip(0.25 + 0.75 * jax.random.uniform(key_of[2], (TOKENS, TOP), jnp.float32) ** level_of(key_of[2], (TOKENS, TOP), ((0, 256),), -0.2, 0.2), 0.25, 1.0)
    cotangent = noise(key_of[3], (TOKENS, D), 1.0, 6.0, ((0, 256),))
    gate_weight = noise(key_of[4], (EXPERTS, FF, D), D ** -0.5, 0.21875, ((0, 16), (1, 16)))
    up_weight = noise(key_of[5], (EXPERTS, FF, D), D ** -0.5, 0.21875, ((0, 16), (1, 16)))
    down_weight = noise(key_of[6], (EXPERTS, FF, D), FF ** -0.5, 0.109375, ((0, 16), (1, 16)))
    return {"tokens": tokens, "routes": routes, "route_gates": route_gates, "cotangent": cotangent, "gate_weight": gate_weight, "up_weight": up_weight, "down_weight": down_weight}


def slot_numbers(block_routes):
    flat_routes = block_routes.reshape(-1)
    labels = jnp.arange(EXPERTS, dtype=jnp.int32)
    hit_table = (flat_routes[:, None] == labels[None, :]).astype(jnp.int32)
    before = jnp.cumsum(hit_table, axis=0) - hit_table
    return (flat_routes * CAP + jnp.sum(before * hit_table, axis=1)).astype(jnp.int32)


def place_rows(block_rows, block_slots):
    blank_rows = jnp.zeros((EXPERTS * CAP, D), jnp.bfloat16)
    return blank_rows.at[block_slots].set(block_rows)


def pick_rows(block_buffer, block_slots):
    return block_buffer[block_slots]


def expert_pass(token_rows, grad_rows, w_gate, w_up, w_down):
    pre_gate = jnp.dot(token_rows, w_gate.T, preferred_element_type=jnp.float32)
    pre_up = jnp.dot(token_rows, w_up.T, preferred_element_type=jnp.float32)
    sigmoid_gate = jax.nn.sigmoid(pre_gate)
    active = pre_gate * sigmoid_gate
    silu_slope = sigmoid_gate * (1.0 + pre_gate * (1.0 - sigmoid_gate))
    hidden = (active * pre_up).astype(jnp.bfloat16)
    expert_out = jnp.dot(hidden, w_down, preferred_element_type=jnp.float32).astype(jnp.bfloat16)
    grad_hidden = jnp.dot(grad_rows, w_down.T, preferred_element_type=jnp.float32)
    grad_gate = (grad_hidden * pre_up * silu_slope).astype(jnp.bfloat16)
    grad_up = (grad_hidden * active).astype(jnp.bfloat16)
    grad_input = (jnp.dot(grad_gate, w_gate, preferred_element_type=jnp.float32)
                  + jnp.dot(grad_up, w_up, preferred_element_type=jnp.float32)).astype(jnp.bfloat16)
    gate_term = jnp.dot(grad_gate.T, token_rows, preferred_element_type=jnp.float32)
    up_term = jnp.dot(grad_up.T, token_rows, preferred_element_type=jnp.float32)
    down_term = jnp.dot(hidden.T, grad_rows, preferred_element_type=jnp.float32)
    return expert_out, grad_input, gate_term, up_term, down_term


def rounded_add(total, term):
    return total + lax.optimization_barrier(term.astype(jnp.bfloat16)).astype(jnp.float32)


def reference(tokens, routes, route_gates, cotangent, gate_weight, up_weight, down_weight):
    blocks = N_DP * N_EXPERT
    slot_ids = jax.vmap(slot_numbers)(routes.reshape(blocks, TOK_DEV, TOP))
    token_copies = jnp.repeat(tokens.reshape(blocks, TOK_DEV, D), TOP, axis=1)
    gate_table = route_gates.reshape(blocks, TOK_DEV, TOP, 1)
    route_cotangent = (cotangent.astype(jnp.float32).reshape(blocks, TOK_DEV, 1, D) * gate_table).astype(jnp.bfloat16)
    route_cotangent = route_cotangent.reshape(blocks, TOK_DEV * TOP, D)
    sent_rows = jax.vmap(place_rows)(token_copies, slot_ids)
    sent_grads = jax.vmap(place_rows)(route_cotangent, slot_ids)

    def regroup(buffer):
        shaped = buffer.reshape(N_DP, N_EXPERT, EXPERTS, CAP, D)
        return jnp.transpose(shaped, (0, 2, 1, 3, 4)).reshape(N_DP, EXPERTS, N_EXPERT * CAP, D)

    def ungroup(buffer):
        shaped = buffer.reshape(N_DP, EXPERTS, N_EXPERT, CAP, D)
        return jnp.transpose(shaped, (0, 2, 1, 3, 4)).reshape(blocks, EXPERTS * CAP, D)

    def data_row(totals, item):
        expert_rows, expert_grads = item
        results = jax.vmap(expert_pass)(expert_rows, expert_grads, gate_weight, up_weight, down_weight)
        expert_out, grad_input, gate_term, up_term, down_term = results
        totals = (rounded_add(totals[0], gate_term), rounded_add(totals[1], up_term), rounded_add(totals[2], down_term))
        return totals, (expert_out, grad_input)

    zero_grads = jnp.zeros((EXPERTS, FF, D), jnp.float32)
    totals, (expert_out, grad_input) = lax.scan(data_row, (zero_grads, zero_grads, zero_grads),
                                                (regroup(sent_rows), regroup(sent_grads)))
    picked = jax.vmap(pick_rows)(ungroup(expert_out), slot_ids).astype(jnp.float32).reshape(blocks, TOK_DEV, TOP, D)
    mixed_output = jnp.sum(gate_table * picked, axis=2).astype(jnp.bfloat16).reshape(TOKENS, D)
    picked_grads = jax.vmap(pick_rows)(ungroup(grad_input), slot_ids).astype(jnp.float32).reshape(blocks, TOK_DEV, TOP, D)
    token_grads = jnp.sum(picked_grads, axis=2).astype(jnp.bfloat16).reshape(TOKENS, D)
    grad_scale = float(TOK_DEV * TOP * N_DP) ** -0.5
    return mixed_output, token_grads, totals[0] * grad_scale, totals[1] * grad_scale, totals[2] * grad_scale
```

```python
import functools

import jax
import jax.numpy as jnp
from jax import lax
from jax.experimental import pallas as pl
from jax.experimental.pallas import tpu as pltpu
from jax.sharding import Mesh, PartitionSpec as P

BF16 = jnp.bfloat16
F32 = jnp.float32
CORES = 2
GROUP = 4
PEAK_PER_US = 1.15e9
FAR_US = 5.0
NEAR_US = 1.0
MERGE_US = 30.0
VMEM_BYTES = 60 * 1024 * 1024


def dot_nn(a, b):
    return lax.dot_general(a, b, (((1,), (0,)), ((), ())), preferred_element_type=F32)


def dot_nt(a, b):
    return lax.dot_general(a, b, (((1,), (1,)), ((), ())), preferred_element_type=F32)


def dot_tn(a, b):
    return lax.dot_general(a, b, (((0,), (0,)), ((), ())), preferred_element_type=F32)


def whole(count):
    return [pl.BlockSpec(memory_space=pltpu.VMEM) for _ in range(count)]


def kernel_call(body, out_shapes, micros, operands, scratch=(), loads=False, stores=0):
    in_hbm = [pl.BlockSpec(memory_space=pl.ANY)]
    return pl.pallas_call(
        body,
        out_shape=out_shapes,
        in_specs=in_hbm * len(operands) if loads else whole(len(operands)),
        out_specs=in_hbm * stores + whole(len(out_shapes) - stores),
        scratch_shapes=list(scratch),
        compiler_params=pltpu.CompilerParams(vmem_limit_bytes=VMEM_BYTES),
        cost_estimate=pl.CostEstimate(
            flops=int(micros * PEAK_PER_US), bytes_accessed=0, transcendentals=0
        ),
    )(*operands)


def start_copy(src, dst, sem):
    copy = pltpu.make_async_copy(src, dst, sem)
    copy.start()
    return copy


def route_info(routes, gates_row, experts, stride):
    tokens = routes.shape[1]
    routes = [routes[k : k + 1, :] for k in range(2)]
    expert_ids = lax.broadcasted_iota(jnp.int32, (experts, tokens), 0)
    hits = [(expert_ids == r).astype(F32) for r in routes]
    row = lax.broadcasted_iota(jnp.int32, (tokens, tokens), 0)
    col = lax.broadcasted_iota(jnp.int32, (tokens, tokens), 1)
    before = dot_nn((hits[0] + hits[1]).astype(BF16), (row < col).astype(F32).astype(BF16))
    slots, gates = [], []
    for k in range(2):
        rank = jnp.sum(before * hits[k], axis=0, keepdims=True)
        slots.append(routes[k] * stride + rank.astype(jnp.int32))
        gates.append(jnp.sum(jnp.where(row == col, gates_row[k : k + 1, :], 0.0), axis=1, keepdims=True))
    return slots, gates


def pack_info(routes, gates_row, width):
    blank = jnp.zeros((1, width - 2 * routes.shape[1]), F32)
    parts = []
    for k in range(2):
        rest = gates_row[k : k + 1, :]
        for _ in range(3):
            part = rest.astype(BF16).astype(F32)
            parts.append(part)
            rest = rest - part
    first = jnp.concatenate([routes[0:1, :].astype(F32), routes[1:2, :].astype(F32), blank], axis=1)
    second = jnp.concatenate(parts, axis=1)
    return jnp.concatenate([first, second, jnp.zeros((14, width), F32)], axis=0).astype(BF16)


def unpack_info(block, tokens):
    block = block.astype(F32)
    cut = lambda row, i: block[row : row + 1, i * tokens : (i + 1) * tokens]
    routes = jnp.concatenate([cut(0, 0), cut(0, 1)], axis=0).astype(jnp.int32)
    gates = [cut(1, 3 * k) + cut(1, 3 * k + 1) + cut(1, 3 * k + 2) for k in range(2)]
    return routes, jnp.concatenate(gates, axis=0)


def dispatch_body(experts, cap, far, *refs):
    stride = 2 * cap
    if far:
        packed_ref, out_ref = refs
        tokens = packed_ref.shape[0] // 2 - 8
        routes, gates_row = unpack_info(packed_ref[2 * tokens :, :], tokens)
        own = packed_ref[:tokens, :]
        cot = packed_ref[tokens : 2 * tokens, :]
    else:
        routes_ref, gates_ref, tokens_ref, cot_ref, *w_refs, out_ref, packed_ref, shard_ref = refs
        tokens, width = tokens_ref.shape
        routes, gates_row = routes_ref[...], gates_ref[...]
        own, cot = tokens_ref[...], cot_ref[...]
        part = w_refs[0].shape[1] // 2
        for half in range(2):
            for m, ref in enumerate(w_refs):
                to = (3 * half + m) * part
                shard_ref[to : to + part, :] = ref[0, half * part : (half + 1) * part, :]
        packed_ref[:tokens, :] = own
        packed_ref[tokens : 2 * tokens, :] = cot
        packed_ref[2 * tokens :, :] = pack_info(routes, gates_row, width)
    slots, gates = route_info(routes, gates_row, experts, stride)
    row_ids = lax.broadcasted_iota(jnp.int32, (experts * stride, tokens), 0)
    gated = [(cot.astype(F32) * gates[k]).astype(BF16) for k in range(2)]
    place_x = ((row_ids == slots[0]) | (row_ids == slots[1])).astype(F32).astype(BF16)
    place_g = [(row_ids == slots[k] + cap).astype(F32).astype(BF16) for k in range(2)]
    left = jnp.concatenate([place_x] + place_g, axis=1)
    right = jnp.concatenate([own] + gated, axis=0)
    out_ref[...] = dot_nn(left, right).astype(BF16)


def combine_body(experts, cap, far, *refs):
    stride = 2 * cap
    if far:
        packed_ref, rows_ref, both_ref = refs
        tokens = both_ref.shape[0] // 2
        routes, gates_row = unpack_info(packed_ref[2 * tokens :, :], tokens)
    else:
        routes_ref, gates_ref, rows_ref, share_ref, mixed_ref, grads_ref = refs
        tokens = mixed_ref.shape[0]
        routes, gates_row = routes_ref[...], gates_ref[...]
    slots, gates = route_info(routes, gates_row, experts, stride)
    row_ids = lax.broadcasted_iota(jnp.int32, (experts * stride, tokens), 0)
    rows = rows_ref[...]
    pick = [(row_ids == slots[k]).astype(F32).astype(BF16) for k in range(2)]
    pick_g = ((row_ids == slots[0] + cap) | (row_ids == slots[1] + cap)).astype(F32).astype(BF16)
    mixed = gates[0] * dot_tn(pick[0], rows) + gates[1] * dot_tn(pick[1], rows)
    grads = dot_tn(pick_g, rows)
    if far:
        both_ref[:tokens, :] = mixed.astype(BF16)
        both_ref[tokens:, :] = grads.astype(BF16)
    else:
        mixed_ref[...] = (mixed + share_ref[:tokens, :].astype(F32)).astype(BF16)
        grads_ref[...] = (grads + share_ref[tokens:, :].astype(F32)).astype(BF16)


def split_matrix(cap):
    size = GROUP * 2 * cap
    out = lax.broadcasted_iota(jnp.int32, (size, size), 0)
    src = lax.broadcasted_iota(jnp.int32, (size, size), 1)
    second = (out >= size // 2).astype(jnp.int32)
    inner = out - second * (size // 2)
    wanted = (inner // cap) * (2 * cap) + inner % cap + second * cap
    return (src == wanted).astype(F32).astype(BF16)


def lane_chunks(size):
    step = 256 if size % 256 == 0 else 384
    return [(at, min(at + step, size)) for at in range(0, size, step)]


def activations(x, g, w_gate, w_up, w_down):
    pre_gate = dot_nt(x, w_gate)
    pre_up = dot_nt(x, w_up)
    grad_hidden = dot_nt(g, w_down)
    sig = jax.nn.sigmoid(pre_gate)
    active = pre_gate * sig
    slope = sig * (1.0 + pre_gate * (1.0 - sig))
    return (
        (active * pre_up).astype(BF16),
        (grad_hidden * pre_up * slope).astype(BF16),
        (grad_hidden * active).astype(BF16),
    )


def piece_cuts(refs, part):
    cuts, to = [], 0
    for number, ref in enumerate(refs):
        for at in range(0, ref.shape[0], 3 * part):
            cuts += [(number, at + m * part, m, to) for m in range(3)]
            to += part
    return cuts


def rows_body(cap, part, raw, last, pieces, *refs):
    refs = list(refs)

    def take(number):
        taken = refs[:number]
        del refs[:number]
        return taken

    given = take(2 if raw else 4)
    w_refs = take(pieces)
    acts_out = take(3)
    kept_out = take(2) if raw else None
    results = take(2)
    loaded, w_all, acts = take(3)
    kept = take(1)[0] if raw else loaded
    sums = take(0 if raw else 2)
    load_sems, w_sems, sum_sems, acts_sems, kept_sems = take(5)
    loads = [start_copy(given[i], loaded.at[i], load_sems.at[i]) for i in range(2)]
    w_loads = []
    for index, (number, row, m, to) in enumerate(piece_cuts(w_refs, part)):
        src = w_refs[number].at[pl.ds(row, part), :]
        w_loads.append(start_copy(src, w_all.at[m, pl.ds(to, part), :], w_sems.at[index]))
    if not raw:
        sum_loads = [start_copy(given[2 + i], sums[i], sum_sems.at[i]) for i in range(2)]
    stores = []
    total = loaded.shape[1]
    half = total // 2
    block = GROUP * 2 * cap
    split = split_matrix(cap)
    for index in range(2):
        loads[index].wait()
        if raw:
            for at in range(0, total, block):
                parted = dot_nn(split, loaded[index, at : at + block, :]).astype(BF16)
                to = index * half + at // 2
                for i in range(2):
                    kept[i, to : to + block // 2, :] = parted[i * block // 2 : (i + 1) * block // 2]
    if raw:
        stores += [start_copy(kept.at[i], kept_out[i], kept_sems.at[i]) for i in range(2)]
    for copy in w_loads:
        copy.wait()
    for lo, hi in lane_chunks(w_all.shape[1]):
        values = activations(
            kept[0], kept[1], w_all[0, lo:hi, :], w_all[1, lo:hi, :], w_all[2, lo:hi, :]
        )
        for m in range(3):
            acts[m, :, lo:hi] = values[m]
    stores += [start_copy(acts.at[m], acts_out[m], acts_sems.at[m]) for m in range(3)]
    out = dot_nn(acts[0], w_all[2])
    grad_in = dot_nn(acts[1], w_all[0]) + dot_nn(acts[2], w_all[1])
    if not raw:
        for copy in sum_loads:
            copy.wait()
        out = out + sums[0][...]
        grad_in = grad_in + sums[1][...]
    if last:
        for index, ref in enumerate(results):
            for at in range(0, total, block):
                rows = slice(index * half + at // 2, index * half + (at + block) // 2)
                both = jnp.concatenate([out[rows, :], grad_in[rows, :]], axis=0).astype(BF16)
                ref[at : at + block, :] = dot_tn(split, both).astype(BF16)
    else:
        results[0][...] = out
        results[1][...] = grad_in
    for copy in stores:
        copy.wait()


def rows_call(cap, part, last, given, pieces, micros):
    raw = len(given) == 2
    total, width = given[0].shape
    count = len(pieces)
    size = sum(p.shape[0] for p in pieces) // 3
    row16 = jax.ShapeDtypeStruct((total, width), BF16)
    row32 = jax.ShapeDtypeStruct((total, width), F32)
    shapes = [jax.ShapeDtypeStruct((total, size), BF16)] * 3
    shapes += [row16] * (2 if raw else 0)
    shapes += [row16 if last else row32] * 2
    scratch = [pltpu.VMEM((2, total, width), BF16), pltpu.VMEM((3, size, width), BF16)]
    scratch += [pltpu.VMEM((3, total, size), BF16)]
    scratch += [pltpu.VMEM((2, total, width), BF16)] if raw else [pltpu.VMEM((total, width), F32)] * 2
    scratch += [pltpu.SemaphoreType.DMA((n,)) for n in (2, 6 * count, 2, 3, 2)]
    body = functools.partial(rows_body, cap, part, raw, last, count)
    operands = list(given) + list(pieces)
    results = kernel_call(body, shapes, micros, operands, scratch, True, 5 if raw else 3)
    return results[:3], results[3:-2], results[-2:]


def terms_body(part, pieces, *refs):
    rows_in, acts_in, t_out = refs[:4], refs[4:13], refs[13 : 13 + pieces]
    rows, near_a, near_b, far, t_all, row_sems, act_sems, t_sems = refs[13 + pieces :]
    size = far.shape[2]
    edge = near_a.shape[2]
    order = ((1, 0), (2, 0), (0, 1))
    row_loads, act_loads = {}, {}
    for m, (act, kind) in enumerate(order):
        if kind not in row_loads:
            row_loads[kind] = [
                start_copy(rows_in[2 * i + kind], rows.at[2 * i + kind], row_sems.at[2 * i + kind])
                for i in range(2)
            ]
        act_loads[m] = [
            start_copy(acts_in[3 * i + act], dst.at[act], act_sems.at[3 * i + act])
            for i, dst in enumerate((near_a, near_b, far))
        ]
    stores = []
    for m, (act, kind) in enumerate(order):
        for copy in row_loads.pop(kind, []) + act_loads[m]:
            copy.wait()
        for lo in range(0, size, 256):
            hi = min(lo + 256, size)
            parts = []
            if lo < edge:
                parts.append(dot_tn(near_a[act, :, lo : min(hi, edge)], rows[kind]))
            if hi > edge:
                parts.append(dot_tn(near_b[act, :, max(lo, edge) - edge : hi - edge], rows[kind]))
            near = parts[0] if len(parts) == 1 else jnp.concatenate(parts, axis=0)
            t_all[m, lo:hi, :] = (near + dot_tn(far[act, :, lo:hi], rows[2 + kind])).astype(BF16)
        for index, (number, row, which, at) in enumerate(piece_cuts(t_out, part)):
            if which == m:
                src = t_all.at[m, pl.ds(at, part), :]
                stores.append(start_copy(src, t_out[number].at[pl.ds(row, part), :], t_sems.at[index]))
    for copy in stores:
        copy.wait()


def terms_call(part, rows, acts, pieces, micros):
    total, width = rows[0].shape
    sizes = [a[0].shape[1] for a in acts]
    shapes = [jax.ShapeDtypeStruct(p.shape, BF16) for p in pieces]
    scratch = [pltpu.VMEM((4, total, width), BF16)]
    scratch += [pltpu.VMEM((3, total, n), BF16) for n in sizes]
    scratch += [pltpu.VMEM((3, sizes[2], width), BF16)]
    scratch += [pltpu.SemaphoreType.DMA((n,)) for n in (4, 9, 6 * len(pieces))]
    operands = list(rows) + [a for group in acts for a in group]
    body = functools.partial(terms_body, part, len(pieces))
    return kernel_call(body, shapes, micros, operands, scratch, True, len(pieces))


def final_body(scale, *refs):
    inputs, outputs = refs[:3], refs[3:]
    part = inputs[0].shape[0] // 6
    for half in range(2):
        for m in range(3):
            rows = slice((3 * half + m) * part, (3 * half + m + 1) * part)
            total = sum(ref[rows, :].astype(F32) for ref in inputs)
            outputs[m][0, half * part : (half + 1) * part, :] = total * scale


def rounded_sum(a, b):
    return (a.astype(F32) + b.astype(F32)).astype(BF16)


def per_device(tokens, routes, route_gates, cotangent, gate_weight, up_weight, down_weight):
    experts = lax.axis_size("expert")
    ring = lax.axis_size("z")
    tok_rows, width = tokens.shape
    choose = routes.shape[1]
    cap = tok_rows * choose * 5 // (4 * experts)
    rows = experts * 2 * cap
    hidden = gate_weight.shape[1]

    def along(value, step):
        return lax.ppermute(value, "z", [(i, (i + step) % ring) for i in range(ring)])

    def opposite(value):
        return along(value, ring // 2)

    def other_core(value):
        return lax.ppermute(value, "core", [(0, 1), (1, 0)])

    def exchange(value):
        moved = lax.all_to_all(
            value.reshape(experts, 2 * cap, width), "expert", split_axis=0, concat_axis=0, tiled=True
        )
        return moved.reshape(rows, width)

    def after(value, *others):
        return lax.optimization_barrier((value, *others))[0]

    def dispatch(micros, far, *given):
        sent = jax.ShapeDtypeStruct((rows, width), BF16)
        packed = jax.ShapeDtypeStruct((2 * tok_rows + 16, width), BF16)
        shard = jax.ShapeDtypeStruct((3 * hidden, width), BF16)
        body = functools.partial(dispatch_body, experts, cap, far)
        return kernel_call(body, [sent] if far else [sent, packed, shard], micros, given)

    def summed(outs):
        return rounded_sum(outs[0], other_core(outs[1]))

    def combine(micros, far, info, sums, share=()):
        returned = exchange(sums)
        one = jax.ShapeDtypeStruct((tok_rows, width), BF16)
        both = jax.ShapeDtypeStruct((2 * tok_rows, width), BF16)
        body = functools.partial(combine_body, experts, cap, far)
        return kernel_call(body, [both] if far else [one] * 2, micros, (*info, returned, *share))

    near_info = (routes.T, route_gates.T)
    near_sent, packed, own = dispatch(
        2.0, False, *near_info, tokens, cotangent, gate_weight, up_weight, down_weight
    )
    far_packed = opposite(packed)
    near = exchange(near_sent)

    part = hidden // 2
    left, right = along(own, 1), along(own, -1)
    far_left, far_right = along(left[: 3 * part], 1), along(right[3 * part :], -1)

    far_sent = dispatch(FAR_US, True, far_packed)[0]
    far = exchange(after(far_sent, near))
    near_swapped = other_core(after(near, far_sent, left))
    near_a, near_rows, near_sums = rows_call(cap, part, False, (near, near_swapped), [own, left], NEAR_US)
    far = after(far, near_sums[0], far_left, far_right)
    pieces = [own, left, right, far_left, far_right]
    far_acts, far_rows, far_outs = rows_call(cap, part, True, (far, other_core(far)), pieces, 10.0)
    near_sums = [after(a, far_outs[0]) for a in near_sums]
    far_outs = summed(far_outs)
    near_b, _, near_outs = rows_call(cap, part, True, (*near_rows, *near_sums), pieces[2:], 6.0)
    t_own, t_left, t_right, t_far_left, t_far_right = terms_call(
        part, (*near_rows, *far_rows), (near_a, [after(a, far_outs) for a in near_b], far_acts), pieces, 7.0
    )

    from_right = along(t_far_left, -1)
    from_left = along(t_far_right, 1)
    to_left = jnp.concatenate([rounded_sum(t_left[: 3 * part], from_right), t_left[3 * part :]])
    to_right = jnp.concatenate([t_right[: 3 * part], rounded_sum(t_right[3 * part :], from_left)])
    scale = float(tok_rows * choose * ring * CORES) ** (-0.5)
    grads = kernel_call(
        functools.partial(final_body, scale),
        [jax.ShapeDtypeStruct((1, hidden, width), F32)] * 3,
        2.0,
        (t_own, along(to_left, -1), along(to_right, 1)),
    )

    far_share = combine(MERGE_US, True, (far_packed,), far_outs)[0]
    near_outs = after(summed(near_outs), far_share)
    mixed, token_grads = combine(2.0, False, near_info, near_outs, (opposite(far_share),))
    return (mixed, token_grads, *grads)


def solution(mesh):
    data, experts = mesh.shape["dp"], mesh.shape["expert"]
    fine = Mesh(mesh.devices.reshape(data // CORES, CORES, experts), ("z", "core", "expert"))
    by_token = P(("z", "core", "expert"), None)
    by_weight = P("expert", ("z", "core"), None)
    return jax.shard_map(
        per_device,
        mesh=fine,
        in_specs=(by_token, by_token, by_token, by_token, by_weight, by_weight, by_weight),
        out_specs=(by_token, by_token, by_weight, by_weight, by_weight),
        check_vma=False,
    )
```

```python
import functools

import jax
import jax.numpy as jnp
from jax import lax
from jax.experimental import pallas as pl
from jax.experimental.pallas import tpu as pltpu
from jax.sharding import Mesh, PartitionSpec as P

BF16 = jnp.bfloat16
F32 = jnp.float32
CORES = 2
GROUP = 4
ROW_STEP = 64
PEAK_PER_US = 1.15e9
FAR_US = 5.0
NEAR_US = 20.0
MERGE_US = 30.0
SHARE_US = 10.0
LATE_US = 8.0
EARLY_US = 8.0
VMEM_BYTES = 60 * 1024 * 1024


def dot_nn(a, b):
    return lax.dot_general(a, b, (((1,), (0,)), ((), ())), preferred_element_type=F32)


def dot_nt(a, b):
    return lax.dot_general(a, b, (((1,), (1,)), ((), ())), preferred_element_type=F32)


def dot_tn(a, b):
    return lax.dot_general(a, b, (((0,), (0,)), ((), ())), preferred_element_type=F32)


def whole(count):
    return [pl.BlockSpec(memory_space=pltpu.VMEM) for _ in range(count)]


def kernel_call(body, out_shapes, micros, operands, scratch=(), loads=0, stores=0):
    in_hbm = [pl.BlockSpec(memory_space=pltpu.HBM)]
    return pl.pallas_call(
        body,
        out_shape=out_shapes,
        in_specs=whole(len(operands) - loads) + in_hbm * loads,
        out_specs=in_hbm * stores + whole(len(out_shapes) - stores),
        scratch_shapes=list(scratch),
        compiler_params=pltpu.CompilerParams(vmem_limit_bytes=VMEM_BYTES),
        cost_estimate=pl.CostEstimate(
            flops=int(micros * PEAK_PER_US), bytes_accessed=0, transcendentals=0
        ),
    )(*operands)


def start_copy(src, dst, sem):
    copy = pltpu.make_async_copy(src, dst, sem)
    copy.start()
    return copy


def route_info(routes, gates_row, experts, stride):
    tokens = routes.shape[1]
    routes = [routes[k : k + 1, :] for k in range(2)]
    expert_ids = lax.broadcasted_iota(jnp.int32, (experts, tokens), 0)
    hits = [(expert_ids == r).astype(F32) for r in routes]
    row = lax.broadcasted_iota(jnp.int32, (tokens, tokens), 0)
    col = lax.broadcasted_iota(jnp.int32, (tokens, tokens), 1)
    before = dot_nn((hits[0] + hits[1]).astype(BF16), (row < col).astype(F32).astype(BF16))
    slots, gates = [], []
    for k in range(2):
        rank = jnp.sum(before * hits[k], axis=0, keepdims=True)
        slots.append(routes[k] * stride + rank.astype(jnp.int32))
        gates.append(jnp.sum(jnp.where(row == col, gates_row[k : k + 1, :], 0.0), axis=1, keepdims=True))
    return slots, gates


def pack_info(routes, gates_row, width):
    blank = jnp.zeros((1, width - 2 * routes.shape[1]), F32)
    parts = []
    for k in range(2):
        rest = gates_row[k : k + 1, :]
        for _ in range(3):
            part = rest.astype(BF16).astype(F32)
            parts.append(part)
            rest = rest - part
    first = jnp.concatenate([routes[0:1, :].astype(F32), routes[1:2, :].astype(F32), blank], axis=1)
    second = jnp.concatenate(parts, axis=1)
    return jnp.concatenate([first, second, jnp.zeros((14, width), F32)], axis=0).astype(BF16)


def unpack_info(block, tokens):
    block = block.astype(F32)
    cut = lambda row, i: block[row : row + 1, i * tokens : (i + 1) * tokens]
    routes = jnp.concatenate([cut(0, 0), cut(0, 1)], axis=0).astype(jnp.int32)
    gates = [cut(1, 3 * k) + cut(1, 3 * k + 1) + cut(1, 3 * k + 2) for k in range(2)]
    return routes, jnp.concatenate(gates, axis=0)


def dispatch_body(experts, cap, far, *refs):
    stride = 2 * cap
    if far:
        packed_ref, out_ref = refs
        tokens = packed_ref.shape[0] // 2 - 8
        routes, gates_row = unpack_info(packed_ref[2 * tokens :, :], tokens)
        own = packed_ref[:tokens, :]
        cot = packed_ref[tokens : 2 * tokens, :]
    else:
        routes_ref, gates_ref, tokens_ref, cot_ref, *w_refs, out_ref, packed_ref, first_ref, second_ref = refs
        tokens, width = tokens_ref.shape
        routes, gates_row = routes_ref[...], gates_ref[...]
        own, cot = tokens_ref[...], cot_ref[...]
        part = w_refs[0].shape[1] // 2
        for half, half_ref in enumerate((first_ref, second_ref)):
            for m, ref in enumerate(w_refs):
                rows = ref[0, half * part : (half + 1) * part, :]
                half_ref[m * part : (m + 1) * part, :] = rows
        packed_ref[:tokens, :] = own
        packed_ref[tokens : 2 * tokens, :] = cot
        packed_ref[2 * tokens :, :] = pack_info(routes, gates_row, width)
    slots, gates = route_info(routes, gates_row, experts, stride)
    row_ids = lax.broadcasted_iota(jnp.int32, (experts * stride, tokens), 0)
    gated = [(cot.astype(F32) * gates[k]).astype(BF16) for k in range(2)]
    place_x = ((row_ids == slots[0]) | (row_ids == slots[1])).astype(F32).astype(BF16)
    place_g = [(row_ids == slots[k] + cap).astype(F32).astype(BF16) for k in range(2)]
    left = jnp.concatenate([place_x] + place_g, axis=1)
    right = jnp.concatenate([own] + gated, axis=0)
    out_ref[...] = dot_nn(left, right).astype(BF16)


def combine_body(experts, cap, far, *refs):
    stride = 2 * cap
    if far:
        packed_ref, rows_ref, both_ref = refs
        tokens = both_ref.shape[0] // 2
        routes, gates_row = unpack_info(packed_ref[2 * tokens :, :], tokens)
    else:
        routes_ref, gates_ref, rows_ref, *share_refs, mixed_ref, grads_ref = refs
        tokens = mixed_ref.shape[0]
        routes, gates_row = routes_ref[...], gates_ref[...]
    slots, gates = route_info(routes, gates_row, experts, stride)
    row_ids = lax.broadcasted_iota(jnp.int32, (experts * stride, tokens), 0)
    rows = rows_ref[...]
    pick = [(row_ids == slots[k]).astype(F32).astype(BF16) for k in range(2)]
    pick_g = ((row_ids == slots[0] + cap) | (row_ids == slots[1] + cap)).astype(F32).astype(BF16)
    mixed = gates[0] * dot_tn(pick[0], rows) + gates[1] * dot_tn(pick[1], rows)
    grads = dot_tn(pick_g, rows)
    if far:
        both_ref[:tokens, :] = mixed.astype(BF16)
        both_ref[tokens:, :] = grads.astype(BF16)
    else:
        mixed_ref[...] = (mixed + share_refs[0][...]).astype(BF16)
        grads_ref[...] = (grads + share_refs[1][...]).astype(BF16)


def split_matrix(cap):
    size = GROUP * 2 * cap
    out = lax.broadcasted_iota(jnp.int32, (size, size), 0)
    src = lax.broadcasted_iota(jnp.int32, (size, size), 1)
    second = (out >= size // 2).astype(jnp.int32)
    inner = out - second * (size // 2)
    wanted = (inner // cap) * (2 * cap) + inner % cap + second * cap
    return (src == wanted).astype(F32).astype(BF16)


def lane_chunks(size):
    step = 256 if size % 256 == 0 else 384
    return [(at, min(at + step, size)) for at in range(0, size, step)]


def activations(x_ref, g_ref, w_all, acts, lo, hi):
    pre_gate = dot_nt(x_ref[...], w_all[0, lo:hi, :])
    pre_up = dot_nt(x_ref[...], w_all[1, lo:hi, :])
    grad_hidden = dot_nt(g_ref[...], w_all[2, lo:hi, :])
    for at in range(0, x_ref.shape[0], ROW_STEP):
        rows = slice(at, at + ROW_STEP)
        gate, up, grad = pre_gate[rows], pre_up[rows], grad_hidden[rows]
        sig = 0.5 * jnp.tanh(0.5 * gate) + 0.5
        active = gate * sig
        slope = sig + active * (1.0 - sig)
        acts[0, rows, lo:hi] = (active * up).astype(BF16)
        acts[1, rows, lo:hi] = (grad * up * slope).astype(BF16)
        acts[2, rows, lo:hi] = (grad * active).astype(BF16)


def piece_cuts(refs, part):
    cuts, to = [], 0
    for number, ref in enumerate(refs):
        for at in range(0, ref.shape[0], 3 * part):
            cuts += [(number, at + m * part, m, to) for m in range(3)]
            to += part
    return cuts


def merge_rows(cap, out, grad_in, results):
    split = split_matrix(cap)
    block = split.shape[0]
    half = out.shape[0] // 2
    for index, ref in enumerate(results):
        for at in range(0, 2 * half, block):
            rows = slice(index * half + at // 2, index * half + (at + block) // 2)
            both = jnp.concatenate([out[rows, :], grad_in[rows, :]], axis=0).astype(BF16)
            ref[at : at + block, :] = dot_tn(split, both).astype(BF16)


class Pending:
    def __init__(self):
        self.copies = {}

    def add(self, name, src, dst, sem):
        self.copies.setdefault(name, []).append(start_copy(src, dst, sem))

    def pieces(self, w_refs, part, w_all, w_sems, matrix):
        for index, (number, row, m, to) in enumerate(piece_cuts(w_refs, part)):
            if m == matrix:
                src = w_refs[number].at[pl.ds(row, part), :]
                self.add(m, src, w_all.at[m, pl.ds(to, part), :], w_sems.at[index])

    def __call__(self, *names):
        for name in names:
            for copy in self.copies.pop(name, ()):
                copy.wait()


def rows_body(cap, part, last, pieces, *refs):
    given, w_refs, refs = refs[:2], refs[2 : 2 + pieces], refs[2 + pieces :]
    acts_out, kept_out, results = refs[:3], refs[3:5], refs[5:7]
    loaded, w_all, acts, kept, load_sems, w_sems, acts_sems, kept_sems = refs[7:]
    ready = Pending()
    for i in range(2):
        ready.add(("rows", i), given[i], loaded.at[i], load_sems.at[i])
    for m in range(3):
        ready.pieces(w_refs, part, w_all, w_sems, m)
    total = loaded.shape[1]
    half = total // 2
    split = split_matrix(cap)
    block = split.shape[0]
    for index in range(2):
        ready(("rows", index))
        for at in range(0, total, block):
            parted = dot_nn(split, loaded[index, at : at + block, :]).astype(BF16)
            to = index * half + at // 2
            for i in range(2):
                kept[i, to : to + block // 2, :] = parted[i * block // 2 : (i + 1) * block // 2]
    for i in range(2):
        ready.add("out", kept.at[i], kept_out[i], kept_sems.at[i])
    ready(0, 1, 2)
    for lo, hi in lane_chunks(w_all.shape[1]):
        activations(kept.at[0], kept.at[1], w_all, acts, lo, hi)
    for m in range(3):
        ready.add("out", acts.at[m], acts_out[m], acts_sems.at[m])
    out = dot_nn(acts[0], w_all[2])
    grad_in = dot_nn(acts[1], w_all[0]) + dot_nn(acts[2], w_all[1])
    if last:
        merge_rows(cap, out, grad_in, results)
    else:
        results[0][...] = out.astype(BF16)
        results[1][...] = grad_in.astype(BF16)
    ready("out")


def rows_call(cap, part, last, given, pieces, micros):
    total, width = given[0].shape
    count = len(pieces)
    size = count * part
    row16 = jax.ShapeDtypeStruct((total, width), BF16)
    shapes = [jax.ShapeDtypeStruct((total, size), BF16)] * 3 + [row16] * 4
    scratch = [pltpu.VMEM((2, total, width), BF16), pltpu.VMEM((3, size, width), BF16)]
    scratch += [pltpu.VMEM((3, total, size), BF16), pltpu.VMEM((2, total, width), BF16)]
    scratch += [pltpu.SemaphoreType.DMA((n,)) for n in (2, 3 * count, 3, 2)]
    body = functools.partial(rows_body, cap, part, last, count)
    operands = list(given) + list(pieces)
    results = kernel_call(body, shapes, micros, operands, scratch, len(operands), 5)
    return results[:3], results[3:5], results[5:]


def term_group(part, near, far, rows, t_all, t_out, t_sems, ready):
    for m, (act, kind) in enumerate(((1, 0), (2, 0), (0, 1))):
        ready("xg"[kind], "xg"[kind] + "far", ("acts", act))
        for lo, hi in lane_chunks(near.shape[2]):
            term = dot_tn(near[act, :, lo:hi], rows[kind]) + dot_tn(far[act, :, lo:hi], rows[2 + kind])
            t_all[m, lo:hi, :] = term.astype(BF16)
        for index, (which, at, number, row) in enumerate(t_out.cuts):
            if which == m:
                src = t_all.at[m, pl.ds(at, part), :]
                ready.add("out", src, t_out.refs[number].at[pl.ds(row, part), :], t_sems.at[index])


class Outputs:
    def __init__(self, refs, order, part):
        self.refs = refs
        each = refs[0].shape[0] // (3 * part)
        self.cuts = [
            (m, unit * part, place // each, (place % each) * 3 * part + m * part)
            for place, unit in enumerate(order)
            for m in range(3)
        ]


def late_body(part, early, late, order, *refs):
    rows_in, acts_in, w_refs, refs = refs[:4], refs[4:7], refs[7 : 7 + late], refs[7 + late :]
    t_out, acts_out, refs = refs[:2], refs[2:5], refs[5:]
    rows, near, far, w_all, t_all, row_sems, far_sems, w_sems, t_sems, near_sems = refs
    size = near.shape[2]
    ready = Pending()
    ready.add("x", rows_in[0], rows.at[0], row_sems.at[0])
    ready.pieces(w_refs, part, w_all, w_sems, 0)
    ready.pieces(w_refs, part, w_all, w_sems, 1)
    ready.add("g", rows_in[1], rows.at[1], row_sems.at[1])
    ready.pieces(w_refs, part, w_all, w_sems, 2)
    for i, name in ((2, "xfar"), (3, "gfar")):
        ready.add(name, rows_in[i], rows.at[i], row_sems.at[i])
    for act in (1, 2, 0):
        src = acts_in[act].at[:, pl.ds(early * part, size)]
        ready.add(("acts", act), src, far.at[act], far_sems.at[act])
    ready("x", "g", 0, 1, 2)
    for lo, hi in lane_chunks(size):
        activations(rows.at[0], rows.at[1], w_all, near, lo, hi)
    for m in range(3):
        ready.add("out", near.at[m], acts_out[m], near_sems.at[m])
    ready("xfar", "gfar", ("acts", 0), ("acts", 1), ("acts", 2))
    term_group(part, near, far, rows, t_all, Outputs(t_out, order, part), t_sems, ready)
    ready("out")


def late_call(part, rows, acts, early, late, order, micros):
    total, width = rows[0].shape
    count = len(late)
    size = count * part
    row_acts = jax.ShapeDtypeStruct((total, size), BF16)
    shapes = [jax.ShapeDtypeStruct((3 * size // 2, width), BF16)] * 2 + [row_acts] * 3
    scratch = [
        pltpu.VMEM((4, total, width), BF16),
        pltpu.VMEM((3, total, size), BF16),
        pltpu.VMEM((3, total, size), BF16),
        pltpu.VMEM((3, size, width), BF16),
        pltpu.VMEM((3, size, width), BF16),
    ]
    scratch += [pltpu.SemaphoreType.DMA((n,)) for n in (4, 3, 3 * count, 3 * count, 3)]
    operands = [*rows, *acts, *late]
    body = functools.partial(late_body, part, len(early), count, order)
    results = kernel_call(body, shapes, micros, operands, scratch, len(operands), len(shapes))
    return results[:2], results[2:]


def early_body(cap, part, early, late, *refs):
    refs = list(refs)

    def take(number):
        taken = refs[:number]
        del refs[:number]
        return taken

    rows_in, sums_in, near_in, acts_in, more_in, w_refs = (take(n) for n in (4, 2, 3, 3, 3, late))
    t_out, results = take(early), take(2)
    rows, sums, near, far, more, w_all, t_all = take(7)
    row_sems, sum_sems, near_sems, far_sems, more_sems, w_sems, t_sems = refs
    size = near.shape[2]
    ready = Pending()
    for act, kind in ((1, 0), (2, None), (0, 1)):
        if kind is not None:
            for i, name in ((kind, "xg"[kind]), (2 + kind, "xg"[kind] + "far")):
                ready.add(name, rows_in[i], rows.at[i], row_sems.at[i])
        ready.add(("acts", act), near_in[act], near.at[act], near_sems.at[act])
        src = acts_in[act].at[:, pl.ds(0, size)]
        ready.add(("acts", act), src, far.at[act], far_sems.at[act])
    for act, m in ((0, 2), (1, 0), (2, 1)):
        ready.add("more", more_in[act], more.at[act], more_sems.at[act])
        ready.pieces(w_refs, part, w_all, w_sems, m)
    for i in range(2):
        ready.add("more", sums_in[i], sums.at[i], sum_sems.at[i])
    t_out = Outputs(t_out, range(early), part)
    term_group(part, near, far, rows, t_all, t_out, t_sems, ready)
    ready("more", 0, 1, 2)
    merge_rows(
        cap,
        sums[0].astype(F32) + dot_nn(more[0], w_all[2]),
        sums[1].astype(F32) + dot_nn(more[1], w_all[0]) + dot_nn(more[2], w_all[1]),
        results,
    )
    ready("out")


def early_call(cap, part, rows, sums, near, far, more, early, late, micros):
    total, width = rows[0].shape
    size = len(early) * part
    rest = len(late) * part
    row16 = jax.ShapeDtypeStruct((total, width), BF16)
    shapes = [jax.ShapeDtypeStruct(p.shape, BF16) for p in early] + [row16] * 2
    scratch = [
        pltpu.VMEM((4, total, width), BF16),
        pltpu.VMEM((2, total, width), BF16),
        pltpu.VMEM((3, total, size), BF16),
        pltpu.VMEM((3, total, size), BF16),
        pltpu.VMEM((3, total, rest), BF16),
        pltpu.VMEM((3, rest, width), BF16),
        pltpu.VMEM((3, size, width), BF16),
    ]
    scratch += [
        pltpu.SemaphoreType.DMA((n,)) for n in (4, 2, 3, 3, 3, 3 * len(late), 3 * len(early))
    ]
    operands = [*rows, *sums, *near, *far, *more, *late]
    body = functools.partial(early_body, cap, part, len(early), len(late))
    results = kernel_call(body, shapes, micros, operands, scratch, len(operands), len(early))
    return results[: len(early)], results[len(early) :]


def widen_body(given_ref, mixed_ref, grads_ref):
    tokens = mixed_ref.shape[0]
    mixed_ref[...] = given_ref[:tokens, :].astype(F32)
    grads_ref[...] = given_ref[tokens:, :].astype(F32)


def final_body(scale, *refs):
    first, second, left, right, more_left, more_right, *outputs = refs
    part = first.shape[0] // 3
    groups = ((first, 0), (left, 0), (more_right, 3)), ((second, 0), (right, 0), (more_left, 3))
    for half, group in enumerate(groups):
        for m in range(3):
            total = sum(
                ref[(at + m) * part : (at + m + 1) * part, :].astype(F32) for ref, at in group
            )
            outputs[m][0, half * part : (half + 1) * part, :] = total * scale


def rounded_sum(a, b):
    return (a.astype(F32) + b.astype(F32)).astype(BF16)


def per_device(tokens, routes, route_gates, cotangent, gate_weight, up_weight, down_weight):
    experts = lax.axis_size("expert")
    ring = lax.axis_size("z")
    tok_rows, width = tokens.shape
    choose = routes.shape[1]
    cap = tok_rows * choose * 5 // (4 * experts)
    rows = experts * 2 * cap
    hidden = gate_weight.shape[1]
    part = hidden // 2

    def along(value, step):
        return lax.ppermute(value, "z", [(i, (i + step) % ring) for i in range(ring)])

    def opposite(value):
        return along(value, ring // 2)

    def other_core(value):
        return lax.ppermute(value, "core", [(0, 1), (1, 0)])

    def exchange(value):
        moved = lax.all_to_all(
            value.reshape(experts, 2 * cap, width), "expert", split_axis=0, concat_axis=0, tiled=True
        )
        return moved.reshape(rows, width)

    def after(value, *others):
        return lax.optimization_barrier((value, *others))[0]

    def dispatch(micros, far, *given):
        sent = jax.ShapeDtypeStruct((rows, width), BF16)
        packed = jax.ShapeDtypeStruct((2 * tok_rows + 16, width), BF16)
        shard = jax.ShapeDtypeStruct((3 * part, width), BF16)
        body = functools.partial(dispatch_body, experts, cap, far)
        return kernel_call(body, [sent] if far else [sent, packed, shard, shard], micros, given)

    def summed(outs):
        return rounded_sum(outs[0], other_core(outs[1]))

    def combine(micros, far, info, returned, share=()):
        one = jax.ShapeDtypeStruct((tok_rows, width), BF16)
        both = jax.ShapeDtypeStruct((2 * tok_rows, width), BF16)
        body = functools.partial(combine_body, experts, cap, far)
        return kernel_call(body, [both] if far else [one] * 2, micros, (*info, returned, *share))

    near_info = (routes.T, route_gates.T)
    near_sent, packed, first, second = dispatch(
        2.0, False, *near_info, tokens, cotangent, gate_weight, up_weight, down_weight
    )
    far_packed = opposite(packed)
    near = exchange(near_sent)

    left_first, right_second = along(first, 1), along(second, -1)
    far_sent = dispatch(FAR_US, True, far_packed)[0]
    far = exchange(after(far_sent, near, left_first, right_second))
    left_second, right_first = along(second, 1), along(first, -1)
    far_first, far_second = along(left_first, 1), along(right_second, -1)
    early = [first, second, left_first, right_second]
    late = [left_second, right_first, far_first, far_second]

    near_swapped = other_core(after(near, far_sent, left_first, right_second))
    near_a, near_rows, near_sums = rows_call(cap, part, False, (near, near_swapped), early, NEAR_US)
    far = after(far, near_sums[0], *late)
    far_acts, far_rows, far_outs = rows_call(cap, part, True, (far, other_core(far)), early + late, 10.0)
    both_rows = (*near_rows, *far_rows)
    (go_left, go_right), near_b = late_call(
        part, both_rows, far_acts, early, late, (2, 0, 3, 1), LATE_US
    )
    far_outs = summed((after(far_outs[0], near_b[0]), far_outs[1]))
    near_sums = [after(a, far_outs) for a in near_sums]
    early_terms, near_outs = early_call(
        cap, part, both_rows, near_sums, near_a, far_acts, near_b, early, late, EARLY_US
    )
    t_first, t_second, t_left_first, t_right_second = early_terms

    far_share = combine(MERGE_US, True, (far_packed,), exchange(far_outs))[0]
    near_sum = after(summed(near_outs), far_share)
    returned = exchange(near_sum)

    back_first, back_second = along(go_left, -1), along(go_right, 1)
    half = 3 * part
    to_left = along(rounded_sum(t_left_first, back_first[:half]), -1)
    to_right = along(rounded_sum(after(t_right_second, near_sum), back_second[:half]), 1)

    scale = float(tok_rows * choose * ring * CORES) ** (-0.5)
    grads = kernel_call(
        functools.partial(final_body, scale),
        [jax.ShapeDtypeStruct((1, hidden, width), F32)] * 3,
        2.0,
        (after(t_first, returned), t_second, to_left, to_right, back_first, back_second),
    )
    share = kernel_call(
        widen_body, [jax.ShapeDtypeStruct((tok_rows, width), F32)] * 2, SHARE_US, (opposite(far_share),)
    )
    mixed, token_grads = combine(2.0, False, near_info, returned, share)
    return (mixed, token_grads, *grads)


def solution(mesh):
    data, experts = mesh.shape["dp"], mesh.shape["expert"]
    fine = Mesh(mesh.devices.reshape(data // CORES, CORES, experts), ("z", "core", "expert"))
    by_token = P(("z", "core", "expert"), None)
    by_weight = P("expert", ("z", "core"), None)
    return jax.shard_map(
        per_device,
        mesh=fine,
        in_specs=(by_token, by_token, by_token, by_token, by_weight, by_weight, by_weight),
        out_specs=(by_token, by_token, by_weight, by_weight, by_weight),
        check_vma=False,
    )
```

```python
import functools

import jax
import jax.numpy as jnp
from jax import lax
from jax.experimental import pallas as pl
from jax.experimental.pallas import tpu as pltpu
from jax.sharding import Mesh, PartitionSpec as P

BF16 = jnp.bfloat16
F32 = jnp.float32
CORES = 2
GROUP = 4
ROW_STEP = 64
PEAK_PER_US = 1.15e9
FAR_US = 5.0
NEAR_US = 20.0
MERGE_US = 30.0
SHARE_US = 10.0
LATE_US = 8.0
EARLY_US = 8.0
VMEM_BYTES = 60 * 1024 * 1024


def dot_nn(a, b):
    return lax.dot_general(a, b, (((1,), (0,)), ((), ())), preferred_element_type=F32)


def dot_nt(a, b):
    return lax.dot_general(a, b, (((1,), (1,)), ((), ())), preferred_element_type=F32)


def dot_tn(a, b):
    return lax.dot_general(a, b, (((0,), (0,)), ((), ())), preferred_element_type=F32)


def whole(count):
    return [pl.BlockSpec(memory_space=pltpu.VMEM) for _ in range(count)]


def kernel_call(body, out_shapes, micros, operands, scratch=(), loads=0, stores=0):
    in_hbm = [pl.BlockSpec(memory_space=pltpu.HBM)]
    return pl.pallas_call(
        body,
        out_shape=out_shapes,
        in_specs=whole(len(operands) - loads) + in_hbm * loads,
        out_specs=in_hbm * stores + whole(len(out_shapes) - stores),
        scratch_shapes=list(scratch),
        compiler_params=pltpu.CompilerParams(vmem_limit_bytes=VMEM_BYTES),
        cost_estimate=pl.CostEstimate(
            flops=int(micros * PEAK_PER_US), bytes_accessed=0, transcendentals=0
        ),
    )(*operands)


def start_copy(src, dst, sem):
    copy = pltpu.make_async_copy(src, dst, sem)
    copy.start()
    return copy


def route_info(routes, gates_row, experts, stride):
    tokens = routes.shape[1]
    routes = [routes[k : k + 1, :] for k in range(2)]
    expert_ids = lax.broadcasted_iota(jnp.int32, (experts, tokens), 0)
    hits = [(expert_ids == r).astype(F32) for r in routes]
    row = lax.broadcasted_iota(jnp.int32, (tokens, tokens), 0)
    col = lax.broadcasted_iota(jnp.int32, (tokens, tokens), 1)
    before = dot_nn((hits[0] + hits[1]).astype(BF16), (row < col).astype(F32).astype(BF16))
    slots, gates = [], []
    for k in range(2):
        rank = jnp.sum(before * hits[k], axis=0, keepdims=True)
        slots.append(routes[k] * stride + rank.astype(jnp.int32))
        gates.append(jnp.sum(jnp.where(row == col, gates_row[k : k + 1, :], 0.0), axis=1, keepdims=True))
    return slots, gates


def pack_info(routes, gates_row, width):
    blank = jnp.zeros((1, width - 2 * routes.shape[1]), F32)
    parts = []
    for k in range(2):
        rest = gates_row[k : k + 1, :]
        for _ in range(3):
            part = rest.astype(BF16).astype(F32)
            parts.append(part)
            rest = rest - part
    first = jnp.concatenate([routes[0:1, :].astype(F32), routes[1:2, :].astype(F32), blank], axis=1)
    second = jnp.concatenate(parts, axis=1)
    return jnp.concatenate([first, second, jnp.zeros((14, width), F32)], axis=0).astype(BF16)


def unpack_info(block, tokens):
    block = block.astype(F32)
    cut = lambda row, i: block[row : row + 1, i * tokens : (i + 1) * tokens]
    routes = jnp.concatenate([cut(0, 0), cut(0, 1)], axis=0).astype(jnp.int32)
    gates = [cut(1, 3 * k) + cut(1, 3 * k + 1) + cut(1, 3 * k + 2) for k in range(2)]
    return routes, jnp.concatenate(gates, axis=0)


def dispatch_body(experts, cap, far, *refs):
    stride = 2 * cap
    if far:
        packed_ref, out_ref = refs
        tokens = packed_ref.shape[0] // 2 - 8
        routes, gates_row = unpack_info(packed_ref[2 * tokens :, :], tokens)
        own = packed_ref[:tokens, :]
        cot = packed_ref[tokens : 2 * tokens, :]
    else:
        routes_ref, gates_ref, tokens_ref, cot_ref, *w_refs, out_ref, packed_ref, first_ref, second_ref = refs
        tokens, width = tokens_ref.shape
        routes, gates_row = routes_ref[...], gates_ref[...]
        own, cot = tokens_ref[...], cot_ref[...]
        part = w_refs[0].shape[1] // 2
        for half, half_ref in enumerate((first_ref, second_ref)):
            for m, ref in enumerate(w_refs):
                rows = ref[0, half * part : (half + 1) * part, :]
                half_ref[m * part : (m + 1) * part, :] = rows
        packed_ref[:tokens, :] = own
        packed_ref[tokens : 2 * tokens, :] = cot
        packed_ref[2 * tokens :, :] = pack_info(routes, gates_row, width)
    slots, gates = route_info(routes, gates_row, experts, stride)
    row_ids = lax.broadcasted_iota(jnp.int32, (experts * stride, tokens), 0)
    gated = [(cot.astype(F32) * gates[k]).astype(BF16) for k in range(2)]
    place_x = ((row_ids == slots[0]) | (row_ids == slots[1])).astype(F32).astype(BF16)
    place_g = [(row_ids == slots[k] + cap).astype(F32).astype(BF16) for k in range(2)]
    left = jnp.concatenate([place_x] + place_g, axis=1)
    right = jnp.concatenate([own] + gated, axis=0)
    out_ref[...] = dot_nn(left, right).astype(BF16)


def combine_body(experts, cap, far, *refs):
    stride = 2 * cap
    if far:
        packed_ref, rows_ref, both_ref = refs
        tokens = both_ref.shape[0] // 2
        routes, gates_row = unpack_info(packed_ref[2 * tokens :, :], tokens)
    else:
        routes_ref, gates_ref, rows_ref, *share_refs, mixed_ref, grads_ref = refs
        tokens = mixed_ref.shape[0]
        routes, gates_row = routes_ref[...], gates_ref[...]
    slots, gates = route_info(routes, gates_row, experts, stride)
    row_ids = lax.broadcasted_iota(jnp.int32, (experts * stride, tokens), 0)
    rows = rows_ref[...]
    pick = [(row_ids == slots[k]).astype(F32).astype(BF16) for k in range(2)]
    pick_g = ((row_ids == slots[0] + cap) | (row_ids == slots[1] + cap)).astype(F32).astype(BF16)
    mixed = gates[0] * dot_tn(pick[0], rows) + gates[1] * dot_tn(pick[1], rows)
    grads = dot_tn(pick_g, rows)
    if far:
        both_ref[:tokens, :] = mixed.astype(BF16)
        both_ref[tokens:, :] = grads.astype(BF16)
    else:
        mixed_ref[...] = (mixed + share_refs[0][...]).astype(BF16)
        grads_ref[...] = (grads + share_refs[1][...]).astype(BF16)


def split_matrix(cap):
    size = GROUP * 2 * cap
    out = lax.broadcasted_iota(jnp.int32, (size, size), 0)
    src = lax.broadcasted_iota(jnp.int32, (size, size), 1)
    second = (out >= size // 2).astype(jnp.int32)
    inner = out - second * (size // 2)
    wanted = (inner // cap) * (2 * cap) + inner % cap + second * cap
    return (src == wanted).astype(F32).astype(BF16)


def lane_chunks(size):
    step = 256 if size % 256 == 0 else 384
    return [(at, min(at + step, size)) for at in range(0, size, step)]


def activations(x_ref, g_ref, w_all, acts, lo, hi):
    pre_gate = dot_nt(x_ref[...], w_all[0, lo:hi, :])
    pre_up = dot_nt(x_ref[...], w_all[1, lo:hi, :])
    grad_hidden = dot_nt(g_ref[...], w_all[2, lo:hi, :])
    for at in range(0, x_ref.shape[0], ROW_STEP):
        rows = slice(at, at + ROW_STEP)
        gate, up, grad = pre_gate[rows], pre_up[rows], grad_hidden[rows]
        sig = 0.5 * jnp.tanh(0.5 * gate) + 0.5
        active = gate * sig
        slope = sig + active * (1.0 - sig)
        acts[0, rows, lo:hi] = (active * up).astype(BF16)
        acts[1, rows, lo:hi] = (grad * up * slope).astype(BF16)
        acts[2, rows, lo:hi] = (grad * active).astype(BF16)


def piece_cuts(refs, part):
    cuts, to = [], 0
    for number, ref in enumerate(refs):
        for at in range(0, ref.shape[0], 3 * part):
            cuts += [(number, at + m * part, m, to) for m in range(3)]
            to += part
    return cuts


def merge_rows(cap, out, grad_in, results):
    split = split_matrix(cap)
    block = split.shape[0]
    half = out.shape[0] // 2
    for index, ref in enumerate(results):
        for at in range(0, 2 * half, block):
            rows = slice(index * half + at // 2, index * half + (at + block) // 2)
            both = jnp.concatenate([out[rows, :], grad_in[rows, :]], axis=0).astype(BF16)
            ref[at : at + block, :] = dot_tn(split, both).astype(BF16)


class Pending:
    def __init__(self):
        self.copies = {}

    def add(self, name, src, dst, sem):
        self.copies.setdefault(name, []).append(start_copy(src, dst, sem))

    def pieces(self, w_refs, part, w_all, w_sems, matrix):
        for index, (number, row, m, to) in enumerate(piece_cuts(w_refs, part)):
            if m == matrix:
                src = w_refs[number].at[pl.ds(row, part), :]
                self.add(m, src, w_all.at[m, pl.ds(to, part), :], w_sems.at[index])

    def __call__(self, *names):
        for name in names:
            for copy in self.copies.pop(name, ()):
                copy.wait()


def rows_body(cap, part, last, pieces, *refs):
    given, w_refs, refs = refs[:2], refs[2 : 2 + pieces], refs[2 + pieces :]
    acts_out, kept_out, results = refs[:3], refs[3:5], refs[5:7]
    loaded, w_all, acts, kept, load_sems, w_sems, acts_sems, kept_sems = refs[7:]
    ready = Pending()
    for i in range(2):
        ready.add(("rows", i), given[i], loaded.at[i], load_sems.at[i])
    for m in range(3):
        ready.pieces(w_refs, part, w_all, w_sems, m)
    total = loaded.shape[1]
    half = total // 2
    split = split_matrix(cap)
    block = split.shape[0]
    for index in range(2):
        ready(("rows", index))
        for at in range(0, total, block):
            parted = dot_nn(split, loaded[index, at : at + block, :]).astype(BF16)
            to = index * half + at // 2
            for i in range(2):
                kept[i, to : to + block // 2, :] = parted[i * block // 2 : (i + 1) * block // 2]
    for i in range(2):
        ready.add("out", kept.at[i], kept_out[i], kept_sems.at[i])
    ready(0, 1, 2)
    for lo, hi in lane_chunks(w_all.shape[1]):
        activations(kept.at[0], kept.at[1], w_all, acts, lo, hi)
    for m in range(3):
        ready.add("out", acts.at[m], acts_out[m], acts_sems.at[m])
    out = dot_nn(acts[0], w_all[2])
    grad_in = dot_nn(acts[1], w_all[0]) + dot_nn(acts[2], w_all[1])
    if last:
        merge_rows(cap, out, grad_in, results)
    else:
        results[0][...] = out.astype(BF16)
        results[1][...] = grad_in.astype(BF16)
    ready("out")


def rows_call(cap, part, last, given, pieces, micros):
    total, width = given[0].shape
    count = len(pieces)
    size = count * part
    row16 = jax.ShapeDtypeStruct((total, width), BF16)
    shapes = [jax.ShapeDtypeStruct((total, size), BF16)] * 3 + [row16] * 4
    scratch = [pltpu.VMEM((2, total, width), BF16), pltpu.VMEM((3, size, width), BF16)]
    scratch += [pltpu.VMEM((3, total, size), BF16), pltpu.VMEM((2, total, width), BF16)]
    scratch += [pltpu.SemaphoreType.DMA((n,)) for n in (2, 3 * count, 3, 2)]
    body = functools.partial(rows_body, cap, part, last, count)
    operands = list(given) + list(pieces)
    results = kernel_call(body, shapes, micros, operands, scratch, len(operands), 5)
    return results[:3], results[3:5], results[5:]


def term_group(part, near, far, rows, t_all, t_out, t_sems, ready):
    for m, (act, kind) in enumerate(((1, 0), (2, 0), (0, 1))):
        ready("xg"[kind], "xg"[kind] + "far", ("acts", act))
        for lo, hi in lane_chunks(near.shape[2]):
            term = dot_tn(near[act, :, lo:hi], rows[kind]) + dot_tn(far[act, :, lo:hi], rows[2 + kind])
            t_all[m, lo:hi, :] = term.astype(BF16)
        for index, (which, at, number, row) in enumerate(t_out.cuts):
            if which == m:
                src = t_all.at[m, pl.ds(at, part), :]
                ready.add("out", src, t_out.refs[number].at[pl.ds(row, part), :], t_sems.at[index])


class Outputs:
    def __init__(self, refs, order, part):
        self.refs = refs
        each = refs[0].shape[0] // (3 * part)
        self.cuts = [
            (m, unit * part, place // each, (place % each) * 3 * part + m * part)
            for place, unit in enumerate(order)
            for m in range(3)
        ]


def late_body(part, early, late, order, *refs):
    rows_in, acts_in, w_refs, refs = refs[:4], refs[4:7], refs[7 : 7 + late], refs[7 + late :]
    t_out, acts_out, refs = refs[:2], refs[2:5], refs[5:]
    rows, near, far, w_all, t_all, row_sems, far_sems, w_sems, t_sems, near_sems = refs
    size = near.shape[2]
    ready = Pending()
    ready.add("x", rows_in[0], rows.at[0], row_sems.at[0])
    ready.pieces(w_refs, part, w_all, w_sems, 0)
    ready.pieces(w_refs, part, w_all, w_sems, 1)
    ready.add("g", rows_in[1], rows.at[1], row_sems.at[1])
    ready.pieces(w_refs, part, w_all, w_sems, 2)
    for i, name in ((2, "xfar"), (3, "gfar")):
        ready.add(name, rows_in[i], rows.at[i], row_sems.at[i])
    for act in (1, 2, 0):
        src = acts_in[act].at[:, pl.ds(early * part, size)]
        ready.add(("acts", act), src, far.at[act], far_sems.at[act])
    ready("x", "g", 0, 1, 2)
    for lo, hi in lane_chunks(size):
        activations(rows.at[0], rows.at[1], w_all, near, lo, hi)
    for m in range(3):
        ready.add("out", near.at[m], acts_out[m], near_sems.at[m])
    ready("xfar", "gfar", ("acts", 0), ("acts", 1), ("acts", 2))
    term_group(part, near, far, rows, t_all, Outputs(t_out, order, part), t_sems, ready)
    ready("out")


def late_call(part, rows, acts, early, late, order, micros):
    total, width = rows[0].shape
    count = len(late)
    size = count * part
    row_acts = jax.ShapeDtypeStruct((total, size), BF16)
    shapes = [jax.ShapeDtypeStruct((3 * size // 2, width), BF16)] * 2 + [row_acts] * 3
    scratch = [
        pltpu.VMEM((4, total, width), BF16),
        pltpu.VMEM((3, total, size), BF16),
        pltpu.VMEM((3, total, size), BF16),
        pltpu.VMEM((3, size, width), BF16),
        pltpu.VMEM((3, size, width), BF16),
    ]
    scratch += [pltpu.SemaphoreType.DMA((n,)) for n in (4, 3, 3 * count, 3 * count, 3)]
    operands = [*rows, *acts, *late]
    body = functools.partial(late_body, part, len(early), count, order)
    results = kernel_call(body, shapes, micros, operands, scratch, len(operands), len(shapes))
    return results[:2], results[2:]


def early_body(cap, part, early, late, *refs):
    refs = list(refs)

    def take(number):
        taken = refs[:number]
        del refs[:number]
        return taken

    rows_in, sums_in, near_in, acts_in, more_in, w_refs = (take(n) for n in (4, 2, 3, 3, 3, late))
    t_out, results = take(early), take(2)
    rows, sums, near, far, more, w_all, t_all = take(7)
    row_sems, sum_sems, near_sems, far_sems, more_sems, w_sems, t_sems = refs
    size = near.shape[2]
    ready = Pending()
    for act, kind in ((1, 0), (2, None), (0, 1)):
        if kind is not None:
            for i, name in ((kind, "xg"[kind]), (2 + kind, "xg"[kind] + "far")):
                ready.add(name, rows_in[i], rows.at[i], row_sems.at[i])
        ready.add(("acts", act), near_in[act], near.at[act], near_sems.at[act])
        src = acts_in[act].at[:, pl.ds(0, size)]
        ready.add(("acts", act), src, far.at[act], far_sems.at[act])
    for act, m in ((0, 2), (1, 0), (2, 1)):
        ready.add("more", more_in[act], more.at[act], more_sems.at[act])
        ready.pieces(w_refs, part, w_all, w_sems, m)
    for i in range(2):
        ready.add("more", sums_in[i], sums.at[i], sum_sems.at[i])
    t_out = Outputs(t_out, range(early), part)
    term_group(part, near, far, rows, t_all, t_out, t_sems, ready)
    ready("more", 0, 1, 2)
    merge_rows(
        cap,
        sums[0].astype(F32) + dot_nn(more[0], w_all[2]),
        sums[1].astype(F32) + dot_nn(more[1], w_all[0]) + dot_nn(more[2], w_all[1]),
        results,
    )
    ready("out")


def early_call(cap, part, rows, sums, near, far, more, early, late, micros):
    total, width = rows[0].shape
    size = len(early) * part
    rest = len(late) * part
    row16 = jax.ShapeDtypeStruct((total, width), BF16)
    shapes = [jax.ShapeDtypeStruct(p.shape, BF16) for p in early] + [row16] * 2
    scratch = [
        pltpu.VMEM((4, total, width), BF16),
        pltpu.VMEM((2, total, width), BF16),
        pltpu.VMEM((3, total, size), BF16),
        pltpu.VMEM((3, total, size), BF16),
        pltpu.VMEM((3, total, rest), BF16),
        pltpu.VMEM((3, rest, width), BF16),
        pltpu.VMEM((3, size, width), BF16),
    ]
    scratch += [
        pltpu.SemaphoreType.DMA((n,)) for n in (4, 2, 3, 3, 3, 3 * len(late), 3 * len(early))
    ]
    operands = [*rows, *sums, *near, *far, *more, *late]
    body = functools.partial(early_body, cap, part, len(early), len(late))
    results = kernel_call(body, shapes, micros, operands, scratch, len(operands), len(early))
    return results[: len(early)], results[len(early) :]


def widen_body(given_ref, mixed_ref, grads_ref):
    tokens = mixed_ref.shape[0]
    mixed_ref[...] = given_ref[:tokens, :].astype(F32)
    grads_ref[...] = given_ref[tokens:, :].astype(F32)


def final_body(scale, *refs):
    first, second, left, right, more_left, more_right, *outputs = refs
    part = first.shape[0] // 3
    groups = ((first, 0), (left, 0), (more_right, 3)), ((second, 0), (right, 0), (more_left, 3))
    for half, group in enumerate(groups):
        for m in range(3):
            total = sum(
                ref[(at + m) * part : (at + m + 1) * part, :].astype(F32) for ref, at in group
            )
            outputs[m][0, half * part : (half + 1) * part, :] = total * scale


def rounded_sum(a, b):
    return (a.astype(F32) + b.astype(F32)).astype(BF16)


def per_device(tokens, routes, route_gates, cotangent, gate_weight, up_weight, down_weight):
    experts = lax.axis_size("expert")
    ring = lax.axis_size("z")
    tok_rows, width = tokens.shape
    choose = routes.shape[1]
    cap = tok_rows * choose * 5 // (4 * experts)
    rows = experts * 2 * cap
    hidden = gate_weight.shape[1]
    part = hidden // 2

    def along(value, step):
        return lax.ppermute(value, "z", [(i, (i + step) % ring) for i in range(ring)])

    def opposite(value):
        return along(value, ring // 2)

    def other_core(value):
        return lax.ppermute(value, "core", [(0, 1), (1, 0)])

    def exchange(value):
        moved = lax.all_to_all(
            value.reshape(experts, 2 * cap, width), "expert", split_axis=0, concat_axis=0, tiled=True
        )
        return moved.reshape(rows, width)

    def after(value, *others):
        return lax.optimization_barrier((value, *others))[0]

    def dispatch(micros, far, *given):
        sent = jax.ShapeDtypeStruct((rows, width), BF16)
        packed = jax.ShapeDtypeStruct((2 * tok_rows + 16, width), BF16)
        shard = jax.ShapeDtypeStruct((3 * part, width), BF16)
        body = functools.partial(dispatch_body, experts, cap, far)
        return kernel_call(body, [sent] if far else [sent, packed, shard, shard], micros, given)

    def summed(outs):
        return rounded_sum(outs[0], other_core(outs[1]))

    def combine(micros, far, info, returned, share=()):
        one = jax.ShapeDtypeStruct((tok_rows, width), BF16)
        both = jax.ShapeDtypeStruct((2 * tok_rows, width), BF16)
        body = functools.partial(combine_body, experts, cap, far)
        return kernel_call(body, [both] if far else [one] * 2, micros, (*info, returned, *share))

    near_info = (routes.T, route_gates.T)
    near_sent, packed, first, second = dispatch(
        2.0, False, *near_info, tokens, cotangent, gate_weight, up_weight, down_weight
    )
    far_packed = opposite(packed)
    near = exchange(near_sent)

    left_first, right_second = along(first, 1), along(second, -1)
    far_sent = dispatch(FAR_US, True, far_packed)[0]
    far = exchange(after(far_sent, left_first, right_second))
    left_second, right_first = along(second, 1), along(first, -1)
    far_first, far_second = along(left_first, 1), along(right_second, -1)
    early = [first, second, left_first, right_second]
    late = [left_second, right_first, far_first, far_second]

    near_swapped = other_core(after(near, far_sent, left_first, right_second))
    near_a, near_rows, near_sums = rows_call(cap, part, False, (near, near_swapped), early, NEAR_US)
    far = after(far, near_sums[0], *late)
    far_acts, far_rows, far_outs = rows_call(cap, part, True, (far, other_core(far)), early + late, 10.0)
    both_rows = (*near_rows, *far_rows)
    (go_left, go_right), near_b = late_call(
        part, both_rows, far_acts, early, late, (2, 0, 3, 1), LATE_US
    )
    far_outs = summed((after(far_outs[0], near_b[0]), far_outs[1]))
    near_sums = [after(a, far_outs) for a in near_sums]
    early_terms, near_outs = early_call(
        cap, part, both_rows, near_sums, near_a, far_acts, near_b, early, late, EARLY_US
    )
    t_first, t_second, t_left_first, t_right_second = early_terms

    far_share = combine(MERGE_US, True, (far_packed,), exchange(far_outs))[0]
    near_sum = after(summed(near_outs), far_share)
    returned = exchange(near_sum)

    back_first, back_second = along(go_left, -1), along(go_right, 1)
    half = 3 * part
    to_left = along(rounded_sum(t_left_first, back_first[:half]), -1)
    to_right = along(rounded_sum(t_right_second, back_second[:half]), 1)

    scale = float(tok_rows * choose * ring * CORES) ** (-0.5)
    grads = kernel_call(
        functools.partial(final_body, scale),
        [jax.ShapeDtypeStruct((1, hidden, width), F32)] * 3,
        2.0,
        (after(t_first, returned), t_second, to_left, to_right, back_first, back_second),
    )
    share = kernel_call(
        widen_body, [jax.ShapeDtypeStruct((tok_rows, width), F32)] * 2, SHARE_US, (opposite(far_share),)
    )
    mixed, token_grads = combine(2.0, False, near_info, returned, share)
    return (mixed, token_grads, *grads)


def solution(mesh):
    data, experts = mesh.shape["dp"], mesh.shape["expert"]
    fine = Mesh(mesh.devices.reshape(data // CORES, CORES, experts), ("z", "core", "expert"))
    by_token = P(("z", "core", "expert"), None)
    by_weight = P("expert", ("z", "core"), None)
    return jax.shard_map(
        per_device,
        mesh=fine,
        in_specs=(by_token, by_token, by_token, by_token, by_weight, by_weight, by_weight),
        out_specs=(by_token, by_token, by_weight, by_weight, by_weight),
        check_vma=False,
    )
```

```python
import functools

import jax
import jax.numpy as jnp
from jax import lax
from jax.experimental import pallas as pl
from jax.experimental.pallas import tpu as pltpu
from jax.sharding import Mesh, PartitionSpec as P

BF16 = jnp.bfloat16
F32 = jnp.float32
CORES = 2
GROUP = 4
ROW_STEP = 64
PEAK_PER_US = 1.15e9
FAR_US = 5.0
NEAR_US = 20.0
MERGE_US = 30.0
SHARE_US = 10.0
LATE_US = 8.0
EARLY_US = 8.0
VMEM_BYTES = 60 * 1024 * 1024


def dot_nn(a, b):
    return lax.dot_general(a, b, (((1,), (0,)), ((), ())), preferred_element_type=F32)


def dot_nt(a, b):
    return lax.dot_general(a, b, (((1,), (1,)), ((), ())), preferred_element_type=F32)


def dot_tn(a, b):
    return lax.dot_general(a, b, (((0,), (0,)), ((), ())), preferred_element_type=F32)


def whole(count):
    return [pl.BlockSpec(memory_space=pltpu.VMEM) for _ in range(count)]


def kernel_call(body, out_shapes, micros, operands, scratch=(), loads=0, stores=0):
    in_hbm = [pl.BlockSpec(memory_space=pltpu.HBM)]
    return pl.pallas_call(
        body,
        out_shape=out_shapes,
        in_specs=whole(len(operands) - loads) + in_hbm * loads,
        out_specs=in_hbm * stores + whole(len(out_shapes) - stores),
        scratch_shapes=list(scratch),
        compiler_params=pltpu.CompilerParams(vmem_limit_bytes=VMEM_BYTES),
        cost_estimate=pl.CostEstimate(
            flops=int(micros * PEAK_PER_US), bytes_accessed=0, transcendentals=0
        ),
    )(*operands)


def start_copy(src, dst, sem):
    copy = pltpu.make_async_copy(src, dst, sem)
    copy.start()
    return copy


def route_info(routes, gates_row, experts, stride):
    tokens = routes.shape[1]
    routes = [routes[k : k + 1, :] for k in range(2)]
    expert_ids = lax.broadcasted_iota(jnp.int32, (experts, tokens), 0)
    hits = [(expert_ids == r).astype(F32) for r in routes]
    row = lax.broadcasted_iota(jnp.int32, (tokens, tokens), 0)
    col = lax.broadcasted_iota(jnp.int32, (tokens, tokens), 1)
    before = dot_nn((hits[0] + hits[1]).astype(BF16), (row < col).astype(F32).astype(BF16))
    slots, gates = [], []
    for k in range(2):
        rank = jnp.sum(before * hits[k], axis=0, keepdims=True)
        slots.append(routes[k] * stride + rank.astype(jnp.int32))
        gates.append(jnp.sum(jnp.where(row == col, gates_row[k : k + 1, :], 0.0), axis=1, keepdims=True))
    return slots, gates


def pack_info(routes, gates_row, width):
    blank = jnp.zeros((1, width - 2 * routes.shape[1]), F32)
    parts = []
    for k in range(2):
        rest = gates_row[k : k + 1, :]
        for _ in range(3):
            part = rest.astype(BF16).astype(F32)
            parts.append(part)
            rest = rest - part
    first = jnp.concatenate([routes[0:1, :].astype(F32), routes[1:2, :].astype(F32), blank], axis=1)
    second = jnp.concatenate(parts, axis=1)
    return jnp.concatenate([first, second, jnp.zeros((14, width), F32)], axis=0).astype(BF16)


def unpack_info(block, tokens):
    block = block.astype(F32)
    cut = lambda row, i: block[row : row + 1, i * tokens : (i + 1) * tokens]
    routes = jnp.concatenate([cut(0, 0), cut(0, 1)], axis=0).astype(jnp.int32)
    gates = [cut(1, 3 * k) + cut(1, 3 * k + 1) + cut(1, 3 * k + 2) for k in range(2)]
    return routes, jnp.concatenate(gates, axis=0)


def pack_body(routes_ref, gates_ref, tokens_ref, cot_ref, packed_ref):
    tokens, width = tokens_ref.shape
    packed_ref[:tokens, :] = tokens_ref[...]
    packed_ref[tokens : 2 * tokens, :] = cot_ref[...]
    packed_ref[2 * tokens :, :] = pack_info(routes_ref[...], gates_ref[...], width)


def dispatch_body(experts, cap, far, *refs):
    stride = 2 * cap
    if far:
        packed_ref, out_ref = refs
        tokens = packed_ref.shape[0] // 2 - 8
        routes, gates_row = unpack_info(packed_ref[2 * tokens :, :], tokens)
        own = packed_ref[:tokens, :]
        cot = packed_ref[tokens : 2 * tokens, :]
    else:
        routes_ref, gates_ref, tokens_ref, cot_ref, *w_refs, out_ref, first_ref, second_ref = refs
        tokens = tokens_ref.shape[0]
        routes, gates_row = routes_ref[...], gates_ref[...]
        own, cot = tokens_ref[...], cot_ref[...]
        part = w_refs[0].shape[1] // 2
        for half, half_ref in enumerate((first_ref, second_ref)):
            for m, ref in enumerate(w_refs):
                rows = ref[0, half * part : (half + 1) * part, :]
                half_ref[m * part : (m + 1) * part, :] = rows
    slots, gates = route_info(routes, gates_row, experts, stride)
    row_ids = lax.broadcasted_iota(jnp.int32, (experts * stride, tokens), 0)
    gated = [(cot.astype(F32) * gates[k]).astype(BF16) for k in range(2)]
    place_x = ((row_ids == slots[0]) | (row_ids == slots[1])).astype(F32).astype(BF16)
    place_g = [(row_ids == slots[k] + cap).astype(F32).astype(BF16) for k in range(2)]
    left = jnp.concatenate([place_x] + place_g, axis=1)
    right = jnp.concatenate([own] + gated, axis=0)
    out_ref[...] = dot_nn(left, right).astype(BF16)


def combine_body(experts, cap, far, *refs):
    stride = 2 * cap
    if far:
        packed_ref, rows_ref, both_ref = refs
        tokens = both_ref.shape[0] // 2
        routes, gates_row = unpack_info(packed_ref[2 * tokens :, :], tokens)
    else:
        routes_ref, gates_ref, rows_ref, *share_refs, mixed_ref, grads_ref = refs
        tokens = mixed_ref.shape[0]
        routes, gates_row = routes_ref[...], gates_ref[...]
    slots, gates = route_info(routes, gates_row, experts, stride)
    row_ids = lax.broadcasted_iota(jnp.int32, (experts * stride, tokens), 0)
    rows = rows_ref[...]
    pick = [(row_ids == slots[k]).astype(F32).astype(BF16) for k in range(2)]
    pick_g = ((row_ids == slots[0] + cap) | (row_ids == slots[1] + cap)).astype(F32).astype(BF16)
    mixed = gates[0] * dot_tn(pick[0], rows) + gates[1] * dot_tn(pick[1], rows)
    grads = dot_tn(pick_g, rows)
    if far:
        both_ref[:tokens, :] = mixed.astype(BF16)
        both_ref[tokens:, :] = grads.astype(BF16)
    else:
        mixed_ref[...] = (mixed + share_refs[0][...]).astype(BF16)
        grads_ref[...] = (grads + share_refs[1][...]).astype(BF16)


def split_matrix(cap):
    size = GROUP * 2 * cap
    out = lax.broadcasted_iota(jnp.int32, (size, size), 0)
    src = lax.broadcasted_iota(jnp.int32, (size, size), 1)
    second = (out >= size // 2).astype(jnp.int32)
    inner = out - second * (size // 2)
    wanted = (inner // cap) * (2 * cap) + inner % cap + second * cap
    return (src == wanted).astype(F32).astype(BF16)


def lane_chunks(size):
    step = 256 if size % 256 == 0 else 384
    return [(at, min(at + step, size)) for at in range(0, size, step)]


def activations(x_ref, g_ref, w_all, acts, lo, hi):
    pre_gate = dot_nt(x_ref[...], w_all[0, lo:hi, :])
    pre_up = dot_nt(x_ref[...], w_all[1, lo:hi, :])
    grad_hidden = dot_nt(g_ref[...], w_all[2, lo:hi, :])
    for at in range(0, x_ref.shape[0], ROW_STEP):
        rows = slice(at, at + ROW_STEP)
        gate, up, grad = pre_gate[rows], pre_up[rows], grad_hidden[rows]
        sig = 0.5 * jnp.tanh(0.5 * gate) + 0.5
        active = gate * sig
        slope = sig + active * (1.0 - sig)
        acts[0, rows, lo:hi] = (active * up).astype(BF16)
        acts[1, rows, lo:hi] = (grad * up * slope).astype(BF16)
        acts[2, rows, lo:hi] = (grad * active).astype(BF16)


def piece_cuts(refs, part):
    cuts, to = [], 0
    for number, ref in enumerate(refs):
        for at in range(0, ref.shape[0], 3 * part):
            cuts += [(number, at + m * part, m, to) for m in range(3)]
            to += part
    return cuts


def merge_rows(cap, out, grad_in, results):
    split = split_matrix(cap)
    block = split.shape[0]
    half = out.shape[0] // 2
    for index, ref in enumerate(results):
        for at in range(0, 2 * half, block):
            rows = slice(index * half + at // 2, index * half + (at + block) // 2)
            both = jnp.concatenate([out[rows, :], grad_in[rows, :]], axis=0).astype(BF16)
            ref[at : at + block, :] = dot_tn(split, both).astype(BF16)


class Pending:
    def __init__(self):
        self.copies = {}

    def add(self, name, src, dst, sem):
        self.copies.setdefault(name, []).append(start_copy(src, dst, sem))

    def pieces(self, w_refs, part, w_all, w_sems, matrix):
        for index, (number, row, m, to) in enumerate(piece_cuts(w_refs, part)):
            if m == matrix:
                src = w_refs[number].at[pl.ds(row, part), :]
                self.add(m, src, w_all.at[m, pl.ds(to, part), :], w_sems.at[index])

    def __call__(self, *names):
        for name in names:
            for copy in self.copies.pop(name, ()):
                copy.wait()


def rows_body(cap, part, last, pieces, *refs):
    given, w_refs, refs = refs[:2], refs[2 : 2 + pieces], refs[2 + pieces :]
    acts_out, kept_out, results = refs[:3], refs[3:5], refs[5:7]
    loaded, w_all, acts, kept, load_sems, w_sems, acts_sems, kept_sems = refs[7:]
    ready = Pending()
    for i in range(2):
        ready.add(("rows", i), given[i], loaded.at[i], load_sems.at[i])
    for m in range(3):
        ready.pieces(w_refs, part, w_all, w_sems, m)
    total = loaded.shape[1]
    half = total // 2
    split = split_matrix(cap)
    block = split.shape[0]
    for index in range(2):
        ready(("rows", index))
        for at in range(0, total, block):
            parted = dot_nn(split, loaded[index, at : at + block, :]).astype(BF16)
            to = index * half + at // 2
            for i in range(2):
                kept[i, to : to + block // 2, :] = parted[i * block // 2 : (i + 1) * block // 2]
    for i in range(2):
        ready.add("out", kept.at[i], kept_out[i], kept_sems.at[i])
    ready(0, 1, 2)
    for lo, hi in lane_chunks(w_all.shape[1]):
        activations(kept.at[0], kept.at[1], w_all, acts, lo, hi)
    for m in range(3):
        ready.add("out", acts.at[m], acts_out[m], acts_sems.at[m])
    out = dot_nn(acts[0], w_all[2])
    grad_in = dot_nn(acts[1], w_all[0]) + dot_nn(acts[2], w_all[1])
    if last:
        merge_rows(cap, out, grad_in, results)
    else:
        results[0][...] = out.astype(BF16)
        results[1][...] = grad_in.astype(BF16)
    ready("out")


def rows_call(cap, part, last, given, pieces, micros):
    total, width = given[0].shape
    count = len(pieces)
    size = count * part
    row16 = jax.ShapeDtypeStruct((total, width), BF16)
    shapes = [jax.ShapeDtypeStruct((total, size), BF16)] * 3 + [row16] * 4
    scratch = [pltpu.VMEM((2, total, width), BF16), pltpu.VMEM((3, size, width), BF16)]
    scratch += [pltpu.VMEM((3, total, size), BF16), pltpu.VMEM((2, total, width), BF16)]
    scratch += [pltpu.SemaphoreType.DMA((n,)) for n in (2, 3 * count, 3, 2)]
    body = functools.partial(rows_body, cap, part, last, count)
    operands = list(given) + list(pieces)
    results = kernel_call(body, shapes, micros, operands, scratch, len(operands), 5)
    return results[:3], results[3:5], results[5:]


def term_group(part, near, far, rows, t_all, t_out, t_sems, ready):
    for m, (act, kind) in enumerate(((1, 0), (2, 0), (0, 1))):
        ready("xg"[kind], "xg"[kind] + "far", ("acts", act))
        for lo, hi in lane_chunks(near.shape[2]):
            term = dot_tn(near[act, :, lo:hi], rows[kind]) + dot_tn(far[act, :, lo:hi], rows[2 + kind])
            t_all[m, lo:hi, :] = term.astype(BF16)
        for index, (which, at, number, row) in enumerate(t_out.cuts):
            if which == m:
                src = t_all.at[m, pl.ds(at, part), :]
                ready.add("out", src, t_out.refs[number].at[pl.ds(row, part), :], t_sems.at[index])


class Outputs:
    def __init__(self, refs, order, part):
        self.refs = refs
        each = refs[0].shape[0] // (3 * part)
        self.cuts = [
            (m, unit * part, place // each, (place % each) * 3 * part + m * part)
            for place, unit in enumerate(order)
            for m in range(3)
        ]


def late_body(part, early, late, order, *refs):
    rows_in, acts_in, w_refs, refs = refs[:4], refs[4:7], refs[7 : 7 + late], refs[7 + late :]
    t_out, acts_out, refs = refs[:2], refs[2:5], refs[5:]
    rows, near, far, w_all, t_all, row_sems, far_sems, w_sems, t_sems, near_sems = refs
    size = near.shape[2]
    ready = Pending()
    ready.add("x", rows_in[0], rows.at[0], row_sems.at[0])
    ready.pieces(w_refs, part, w_all, w_sems, 0)
    ready.pieces(w_refs, part, w_all, w_sems, 1)
    ready.add("g", rows_in[1], rows.at[1], row_sems.at[1])
    ready.pieces(w_refs, part, w_all, w_sems, 2)
    for i, name in ((2, "xfar"), (3, "gfar")):
        ready.add(name, rows_in[i], rows.at[i], row_sems.at[i])
    for act in (1, 2, 0):
        src = acts_in[act].at[:, pl.ds(early * part, size)]
        ready.add(("acts", act), src, far.at[act], far_sems.at[act])
    ready("x", "g", 0, 1, 2)
    for lo, hi in lane_chunks(size):
        activations(rows.at[0], rows.at[1], w_all, near, lo, hi)
    for m in range(3):
        ready.add("out", near.at[m], acts_out[m], near_sems.at[m])
    ready("xfar", "gfar", ("acts", 0), ("acts", 1), ("acts", 2))
    term_group(part, near, far, rows, t_all, Outputs(t_out, order, part), t_sems, ready)
    ready("out")


def late_call(part, rows, acts, early, late, order, micros):
    total, width = rows[0].shape
    count = len(late)
    size = count * part
    row_acts = jax.ShapeDtypeStruct((total, size), BF16)
    shapes = [jax.ShapeDtypeStruct((3 * size // 2, width), BF16)] * 2 + [row_acts] * 3
    scratch = [
        pltpu.VMEM((4, total, width), BF16),
        pltpu.VMEM((3, total, size), BF16),
        pltpu.VMEM((3, total, size), BF16),
        pltpu.VMEM((3, size, width), BF16),
        pltpu.VMEM((3, size, width), BF16),
    ]
    scratch += [pltpu.SemaphoreType.DMA((n,)) for n in (4, 3, 3 * count, 3 * count, 3)]
    operands = [*rows, *acts, *late]
    body = functools.partial(late_body, part, len(early), count, order)
    results = kernel_call(body, shapes, micros, operands, scratch, len(operands), len(shapes))
    return results[:2], results[2:]


def early_body(cap, part, early, late, *refs):
    refs = list(refs)

    def take(number):
        taken = refs[:number]
        del refs[:number]
        return taken

    rows_in, sums_in, near_in, acts_in, more_in, w_refs = (take(n) for n in (4, 2, 3, 3, 3, late))
    t_out, results = take(early), take(2)
    rows, sums, near, far, more, w_all, t_all = take(7)
    row_sems, sum_sems, near_sems, far_sems, more_sems, w_sems, t_sems = refs
    size = near.shape[2]
    ready = Pending()
    for act, kind in ((1, 0), (2, None), (0, 1)):
        if kind is not None:
            for i, name in ((kind, "xg"[kind]), (2 + kind, "xg"[kind] + "far")):
                ready.add(name, rows_in[i], rows.at[i], row_sems.at[i])
        ready.add(("acts", act), near_in[act], near.at[act], near_sems.at[act])
        src = acts_in[act].at[:, pl.ds(0, size)]
        ready.add(("acts", act), src, far.at[act], far_sems.at[act])
    for act, m in ((0, 2), (1, 0), (2, 1)):
        ready.add("more", more_in[act], more.at[act], more_sems.at[act])
        ready.pieces(w_refs, part, w_all, w_sems, m)
    for i in range(2):
        ready.add("more", sums_in[i], sums.at[i], sum_sems.at[i])
    t_out = Outputs(t_out, range(early), part)
    term_group(part, near, far, rows, t_all, t_out, t_sems, ready)
    ready("more", 0, 1, 2)
    merge_rows(
        cap,
        sums[0].astype(F32) + dot_nn(more[0], w_all[2]),
        sums[1].astype(F32) + dot_nn(more[1], w_all[0]) + dot_nn(more[2], w_all[1]),
        results,
    )
    ready("out")


def early_call(cap, part, rows, sums, near, far, more, early, late, micros):
    total, width = rows[0].shape
    size = len(early) * part
    rest = len(late) * part
    row16 = jax.ShapeDtypeStruct((total, width), BF16)
    shapes = [jax.ShapeDtypeStruct(p.shape, BF16) for p in early] + [row16] * 2
    scratch = [
        pltpu.VMEM((4, total, width), BF16),
        pltpu.VMEM((2, total, width), BF16),
        pltpu.VMEM((3, total, size), BF16),
        pltpu.VMEM((3, total, size), BF16),
        pltpu.VMEM((3, total, rest), BF16),
        pltpu.VMEM((3, rest, width), BF16),
        pltpu.VMEM((3, size, width), BF16),
    ]
    scratch += [
        pltpu.SemaphoreType.DMA((n,)) for n in (4, 2, 3, 3, 3, 3 * len(late), 3 * len(early))
    ]
    operands = [*rows, *sums, *near, *far, *more, *late]
    body = functools.partial(early_body, cap, part, len(early), len(late))
    results = kernel_call(body, shapes, micros, operands, scratch, len(operands), len(early))
    return results[: len(early)], results[len(early) :]


def widen_body(given_ref, mixed_ref, grads_ref):
    tokens = mixed_ref.shape[0]
    mixed_ref[...] = given_ref[:tokens, :].astype(F32)
    grads_ref[...] = given_ref[tokens:, :].astype(F32)


def final_body(scale, *refs):
    first, second, left, right, more_left, more_right, *outputs = refs
    part = first.shape[0] // 3
    groups = ((first, 0), (left, 0), (more_right, 3)), ((second, 0), (right, 0), (more_left, 3))
    for half, group in enumerate(groups):
        for m in range(3):
            total = sum(
                ref[(at + m) * part : (at + m + 1) * part, :].astype(F32) for ref, at in group
            )
            outputs[m][0, half * part : (half + 1) * part, :] = total * scale


def rounded_sum(a, b):
    return (a.astype(F32) + b.astype(F32)).astype(BF16)


def per_device(tokens, routes, route_gates, cotangent, gate_weight, up_weight, down_weight):
    experts = lax.axis_size("expert")
    ring = lax.axis_size("z")
    tok_rows, width = tokens.shape
    choose = routes.shape[1]
    cap = tok_rows * choose * 5 // (4 * experts)
    rows = experts * 2 * cap
    hidden = gate_weight.shape[1]
    part = hidden // 2

    def along(value, step):
        return lax.ppermute(value, "z", [(i, (i + step) % ring) for i in range(ring)])

    def opposite(value):
        return along(value, ring // 2)

    def other_core(value):
        return lax.ppermute(value, "core", [(0, 1), (1, 0)])

    def exchange(value):
        moved = lax.all_to_all(
            value.reshape(experts, 2 * cap, width), "expert", split_axis=0, concat_axis=0, tiled=True
        )
        return moved.reshape(rows, width)

    def after(value, *others):
        return lax.optimization_barrier((value, *others))[0]

    def dispatch(micros, far, *given):
        sent = jax.ShapeDtypeStruct((rows, width), BF16)
        shard = jax.ShapeDtypeStruct((3 * part, width), BF16)
        body = functools.partial(dispatch_body, experts, cap, far)
        return kernel_call(body, [sent] if far else [sent, shard, shard], micros, given)

    def summed(outs):
        return rounded_sum(outs[0], other_core(outs[1]))

    def combine(micros, far, info, returned, share=()):
        one = jax.ShapeDtypeStruct((tok_rows, width), BF16)
        both = jax.ShapeDtypeStruct((2 * tok_rows, width), BF16)
        body = functools.partial(combine_body, experts, cap, far)
        return kernel_call(body, [both] if far else [one] * 2, micros, (*info, returned, *share))

    near_info = (routes.T, route_gates.T)
    packed = jax.ShapeDtypeStruct((2 * tok_rows + 16, width), BF16)
    packed = kernel_call(pack_body, [packed], 1.0, (*near_info, tokens, cotangent))[0]
    near_sent, first, second = dispatch(
        2.0, False, *near_info, tokens, cotangent, gate_weight, up_weight, down_weight
    )
    far_packed = opposite(packed)
    near = exchange(near_sent)

    left_first, right_second = along(first, 1), along(second, -1)
    far_sent = dispatch(FAR_US, True, far_packed)[0]
    far = exchange(after(far_sent, left_first, right_second))
    left_second, right_first = along(second, 1), along(first, -1)
    far_first, far_second = along(left_first, 1), along(right_second, -1)
    early = [first, second, left_first, right_second]
    late = [left_second, right_first, far_first, far_second]

    near_swapped = other_core(after(near, far_sent, left_first, right_second))
    near_a, near_rows, near_sums = rows_call(cap, part, False, (near, near_swapped), early, NEAR_US)
    far = after(far, near_sums[0], *late)
    far_acts, far_rows, far_outs = rows_call(cap, part, True, (far, other_core(far)), early + late, 10.0)
    both_rows = (*near_rows, *far_rows)
    (go_left, go_right), near_b = late_call(
        part, both_rows, far_acts, early, late, (2, 0, 3, 1), LATE_US
    )
    far_outs = summed((after(far_outs[0], near_b[0]), far_outs[1]))
    near_sums = [after(a, far_outs) for a in near_sums]
    early_terms, near_outs = early_call(
        cap, part, both_rows, near_sums, near_a, far_acts, near_b, early, late, EARLY_US
    )
    t_first, t_second, t_left_first, t_right_second = early_terms

    far_share = combine(MERGE_US, True, (far_packed,), exchange(far_outs))[0]
    near_sum = after(summed(near_outs), far_share)
    returned = exchange(near_sum)

    back_first, back_second = along(go_left, -1), along(go_right, 1)
    half = 3 * part
    to_left = along(rounded_sum(t_left_first, back_first[:half]), -1)
    to_right = along(rounded_sum(t_right_second, back_second[:half]), 1)

    scale = float(tok_rows * choose * ring * CORES) ** (-0.5)
    grads = kernel_call(
        functools.partial(final_body, scale),
        [jax.ShapeDtypeStruct((1, hidden, width), F32)] * 3,
        2.0,
        (after(t_first, returned), t_second, to_left, to_right, back_first, back_second),
    )
    share = kernel_call(
        widen_body, [jax.ShapeDtypeStruct((tok_rows, width), F32)] * 2, SHARE_US, (opposite(far_share),)
    )
    mixed, token_grads = combine(2.0, False, near_info, returned, share)
    return (mixed, token_grads, *grads)


def solution(mesh):
    data, experts = mesh.shape["dp"], mesh.shape["expert"]
    fine = Mesh(mesh.devices.reshape(data // CORES, CORES, experts), ("z", "core", "expert"))
    by_token = P(("z", "core", "expert"), None)
    by_weight = P("expert", ("z", "core"), None)
    return jax.shard_map(
        per_device,
        mesh=fine,
        in_specs=(by_token, by_token, by_token, by_token, by_weight, by_weight, by_weight),
        out_specs=(by_token, by_token, by_weight, by_weight, by_weight),
        check_vma=False,
    )
```
